256 devices in a mesh: grp: 2 (over y_hi), row: 16 (over x, y_lo, core), col: 8 (over z).
Axes of the slice: x: 4, y: 4 (y_hi: 2, y_lo: 2; y = y_hi * 2 + y_lo), z: 8, core: 2. Of those that a mesh axis runs over, the one named last changes fastest.
Arguments:
- orbital_b: bfloat16 [4096, 12288], P(('grp', 'row'), 'col'), may hold values from -0.5 to 0.5
- gaps: float32 [4096], P(('grp', 'row')), may hold values from 0.5 to 20
- block_inverse: float32 [1024, 1024], replicated, may hold values from -0.1875 to 0.1875
Outputs:
- sigma: float32 [4096], P(('grp', 'row'))
- w_panel: float32 [8, 1536, 1024], P('col', ('grp', 'row'))
The draws below stay inside these ranges and needn't reach their ends.
All inputs are finite; a program needn't handle non-finite values.
Results may differ from the reference program's by a relative error of at most 0.0028.
Values may be sent and summed in bfloat16 or wider, within the bound.
No kernel may reach another device: no remote copies, remote signals or barrier semaphores. Data moves between devices by JAX's collectives and lax.ppermute only.
A program may use at most 64 MiB of HBM per device.

```python
import math
import jax
import jax.numpy as jnp
from jax import lax

NAUX = 12288
PANEL = 1024
VIRT_DEV = 128
NV = 4096
AUX_DEV = 1536
N_COL = 8


def block_levels(key, dims, pieces, least, high):
    loudness = 1.0
    for dim, parts in pieces:
        draws = jax.random.uniform(jax.random.fold_in(jax.random.fold_in(key, 6), dim), (parts,), jnp.float32, least / len(pieces), high / len(pieces))
        loudness = loudness * jnp.repeat(jnp.exp(draws), dims[dim] // parts).reshape((-1,) + (1,) * (len(dims) - 1 - dim))
    return loudness


def bell_draw(rng, shape, deviation, bound, shards=(), kind=jnp.bfloat16):
    level = block_levels(rng, shape, shards, -0.22, 0.18) if shards else 1.0
    drawn = jax.random.normal(rng, shape, jnp.float32) * deviation * level
    return jnp.minimum(jnp.maximum(drawn, -bound), bound).astype(kind)


def setup_inputs(seed: int = 0) -> dict:
    seeds = jax.random.split(jax.random.key(seed), 4)
    orbital_b = bell_draw(seeds[0], (NV, NAUX), VIRT_DEV ** -0.5, 0.5, ((0, 32), (1, 8)))
    gaps = jnp.clip(jnp.exp(math.log(20.0) - 3.6888795 * jax.random.uniform(seeds[1], (NV,), jnp.float32) ** block_levels(seeds[1], (NV,), ((0, 32),), -0.2, 0.2)), 0.5, 20.0)
    block_inverse = bell_draw(seeds[2], (PANEL, PANEL), PANEL ** -0.5, 0.1875, (), jnp.float32)
    return {"orbital_b": orbital_b, "gaps": gaps, "block_inverse": block_inverse}


def reference(orbital_b, gaps, block_inverse):
    weight = 2.0 * gaps / (gaps * gaps + 1.0)
    panel_b = orbital_b[:, :PANEL]
    weighted = (weight[:, None] * panel_b.astype(jnp.float32)).astype(jnp.bfloat16)
    response = lax.dot_general(orbital_b, weighted, (((0,), (0,)), ((), ())), preferred_element_type=jnp.float32)
    unit = (lax.iota(jnp.int32, NAUX)[:, None] == lax.iota(jnp.int32, PANEL)[None, :]).astype(jnp.float32)
    screened = jnp.dot(unit + response, block_inverse, precision=lax.Precision.HIGHEST)
    screened_low = screened.astype(jnp.bfloat16)
    contracted = jnp.dot(orbital_b, screened_low, preferred_element_type=jnp.float32)
    sigma = -jnp.sum(contracted * panel_b.astype(jnp.float32), axis=1)
    return sigma, screened.reshape(N_COL, AUX_DEV, PANEL)
```

```python
import jax
import jax.numpy as jnp
from jax import lax
from jax.sharding import Mesh, PartitionSpec as P

X, Y, Z, CORE = "x", ("grp", "ylo"), "col", "core"
PLANE = ("grp", "x", "ylo", "core")


def shift(value, axis, size, step):
    return lax.ppermute(value, axis, [(i, (i + step) % size) for i in range(size)])


def spread(panel):
    z = lax.axis_index(Z)
    a = lax.ppermute(panel, Z, [(0, 3)])
    b = lax.ppermute(panel, Z, [(0, 5)])
    held = jnp.where(z == 3, a, jnp.where(z == 5, b, panel))
    a = lax.ppermute(held, Z, [(0, 1), (3, 4), (5, 6)])
    b = lax.ppermute(held, Z, [(0, 7), (3, 2)])
    up = (z == 1) | (z == 4) | (z == 6)
    down = (z == 7) | (z == 2)
    return jnp.where(up, a, jnp.where(down, b, held))


def body(orbital_b, gaps, block_inverse):
    own, width = orbital_b.shape
    panel = block_inverse.shape[0]
    nx, ny = lax.axis_size(X), lax.axis_size(Y)
    x, y, z, core = (lax.axis_index(a) for a in (X, Y, Z, CORE))
    count = width // lax.axis_size(PLANE)
    low, f32 = jnp.bfloat16, jnp.float32

    panels = [spread(orbital_b[:, :panel])]
    blocks = orbital_b.T.reshape(2, nx, -1, own)

    def rows_of(i):
        return lax.dynamic_index_in_dim(blocks, i, 1, False).reshape(-1, own)

    factors = jnp.concatenate(
        [rows_of(x)] + [shift(rows_of((x + k) % nx), X, nx, k) for k in range(1, nx)], axis=1
    )
    gap_list = [gaps] + [shift(gaps, X, nx, k) for k in range(1, nx)]
    half = own // 2
    right = shift(panels[0], X, nx, 1)
    left = shift(panels[0], X, nx, -1)
    far_a = shift(right[:half], X, nx, 1)
    far_b = shift(left[half:], X, nx, -1)
    panels += [right, jnp.concatenate([far_a, far_b], axis=0), left]
    panels = jnp.concatenate(panels, axis=0)
    gap_all = jnp.concatenate(gap_list)
    weight = 2.0 * gap_all / (gap_all * gap_all + 1.0)
    weighted = (weight[:, None] * panels.astype(f32)).astype(low)
    part = jnp.dot(factors, weighted, preferred_element_type=f32)

    part = part.reshape(ny, 2, count, panel)
    kept = lax.dynamic_index_in_dim(part, core, 1, False)
    sent = lax.dynamic_index_in_dim(part, 1 - core, 1, False)
    kept = kept + shift(sent, CORE, 2, 1)
    total = lax.dynamic_index_in_dim(kept, y, 0, False)
    for k in range(1, ny):
        piece = lax.dynamic_index_in_dim(kept, (y + k) % ny, 0, False).astype(low)
        total = total + shift(piece, Y, ny, k).astype(f32)
    first = z * width + lax.axis_index(PLANE) * count
    rows = lax.iota(jnp.int32, count)[:, None] + first
    unit = (rows == lax.iota(jnp.int32, panel)[None, :]).astype(f32)
    screened = jnp.dot(unit + total, block_inverse, precision=lax.Precision.HIGH)

    mine = screened.astype(low)
    gathered = jnp.stack([mine] + [shift(mine, Y, ny, k) for k in range(1, ny)])
    other = shift(gathered, CORE, 2, 1)
    both = jnp.concatenate([gathered, other], axis=0).reshape(-1, panel)
    by_y = factors.reshape(ny, 2, count, -1)
    ordered = jnp.stack(
        [
            lax.dynamic_slice(by_y, ((y - k) % ny, (core + c) % 2, 0, 0), (1, 1, count, nx * own))
            for c in range(2)
            for k in range(ny)
        ]
    ).reshape(-1, nx * own)
    products = lax.dot_general(both, panels, (((1,), (1,)), ((), ())), preferred_element_type=f32)
    local = -jnp.sum(products * ordered.astype(f32), axis=0).reshape(nx, own)
    by_x = jnp.stack([lax.dynamic_index_in_dim(local, (x - i) % nx, 0, False) for i in range(nx)])
    copies = jnp.broadcast_to(by_x[:, None], (nx, lax.axis_size(Z), own)).reshape(-1, own)
    terms = lax.all_to_all(copies, (X, Z), 0, 0, tiled=True)
    sigma = jnp.sum(terms, axis=0)
    return sigma, screened[None]


def solution(mesh):
    split = Mesh(mesh.devices.reshape(2, 4, 2, 2, 8), ("grp", "x", "ylo", "core", "col"))
    return jax.shard_map(
        body,
        mesh=split,
        in_specs=(P(PLANE, Z), P(PLANE), P()),
        out_specs=(P(PLANE), P(Z, PLANE, None)),
        check_vma=False,
    )
```

```python
import jax
import jax.numpy as jnp
from jax import lax
from jax.sharding import Mesh, PartitionSpec as P

X, Y, Z, CORE = "x", ("grp", "ylo"), "col", "core"
PLANE = ("grp", "x", "ylo", "core")
LOW, F32 = jnp.bfloat16, jnp.float32
HOLDER = (0, 0, 0, 0, 0, 1, 1, 1)


def shift(value, axis, size, step):
    return lax.ppermute(value, axis, [(i, (i + step) % size) for i in range(size)])


def along_z(value, pairs):
    return lax.ppermute(value, (CORE, Z), [(b * 8 + a, d * 8 + c) for (a, b), (c, d) in pairs])


def along_x(value, nx, step, target):
    pairs = []
    for x in range(nx):
        for z, core in enumerate(HOLDER):
            source = target if z == 0 else core
            to = (x + step) % nx
            pairs.append(((x * 2 + source) * 8 + z, (to * 2 + target) * 8 + z))
    return lax.ppermute(value, (X, CORE, Z), pairs)


def swap(value):
    return lax.ppermute(value, CORE, [(0, 1), (1, 0)])


def parts_of(value):
    out = []
    for _ in range(3):
        part = lax.reduce_precision(value, 8, 7)
        out.append(part.astype(LOW))
        value = value - part
    return out


def body(orbital_b, gaps, block_inverse):
    own, width = orbital_b.shape
    panel = block_inverse.shape[0]
    nx, ny, nz = lax.axis_size(X), lax.axis_size(Y), lax.axis_size(Z)
    x, y, z, core = (lax.axis_index(a) for a in (X, Y, Z, CORE))
    count = width // lax.axis_size(PLANE)
    is0 = core == 0

    def order(a, b, axis):
        return jnp.concatenate([jnp.where(is0, a, b), jnp.where(is0, b, a)], axis=axis)

    with jax.named_scope("panel_z"):
        piece = orbital_b[:, :panel]
        chip = order(piece, swap(piece), 0)
        far = along_z(chip, [((0, 0), (3, 0)), ((0, 1), (6, 1))])
        near = along_z(chip, [((0, 0), (1, 0)), ((0, 1), (7, 1))])
        next_a = along_z(far, [((3, 0), (4, 0)), ((6, 1), (5, 1))])
        next_b = along_z(far, [((3, 0), (2, 0))])
        chip = jnp.where((z == 3) | (z == 6), far, jnp.where((z == 1) | (z == 7), near, chip))
        chip = jnp.where((z == 4) | (z == 5), next_a, jnp.where(z == 2, next_b, chip))

    with jax.named_scope("blocks"):
        weight = 2.0 * gaps / (gaps * gaps + 1.0)
        rows = orbital_b.T.reshape(2, nx, 2, 2, count, own)
        extra = jnp.concatenate(
            [jnp.stack(parts_of(weight)), jnp.zeros((13, own), LOW)], axis=0
        )
        mine = lax.dynamic_index_in_dim(rows, core, 3, False).reshape(-1, own)
        mine = jnp.concatenate([mine, extra], axis=0)
        sent = lax.dynamic_index_in_dim(rows, 1 - core, 3, False).reshape(-1, own)
        sent = jnp.concatenate([sent, extra], axis=0)
        pair = order(mine, swap(sent), 1)
        blocks = pair[:-16].reshape(2, nx, 2 * count, 2 * own)

        def rows_of(i):
            block = lax.dynamic_index_in_dim(blocks, i, 1, False).reshape(-1, 2 * own)
            return jnp.concatenate([block, pair[-16:]], axis=0)

        b0 = rows_of(x)
        b1, b2, b3 = (shift(rows_of((x + k) % nx), X, nx, k) for k in range(1, nx))
        b2 = order(b2[:, :own], b2[:, own:], 1)
        factors = jnp.concatenate([b0, order(b1, b3, 1), b2], axis=1)
        weight = jnp.sum(factors[-16:-13].astype(F32)[::-1], axis=0)
        factors = factors[:-16]

    with jax.named_scope("panel_x"):
        up = along_x(chip, nx, 1, 0)
        down = along_x(chip, nx, -1, 1)
        first = jnp.where(is0, up, down)
        half = jnp.where(is0, up[:own], down[own:])
        second = lax.ppermute(
            half,
            (X, CORE),
            [(i * 2, (i + 1) % nx * 2) for i in range(nx)]
            + [(i * 2 + 1, (i - 1) % nx * 2 + 1) for i in range(nx)],
        )
        given = along_z(chip, [((i, h), (i, 1 - h)) for i, h in enumerate(HOLDER) if i])
        holder = jnp.where(z >= 5, 1, 0)
        chip = jnp.where((z == 0) | (core == holder), chip, given)
        early = [chip, first, swap(first)]
        late = [second, swap(second)]

    with jax.named_scope("response"):
        start = 0
        part = 0.0
        for group in (early, late):
            block = jnp.concatenate(group, axis=0)
            stop = start + block.shape[0]
            weighted = (weight[start:stop, None] * block.astype(F32)).astype(LOW)
            part = part + jnp.dot(factors[:, start:stop], weighted, preferred_element_type=F32)
            start = stop

    with jax.named_scope("sum_y"):
        kept = part.reshape(ny, count, panel)
        total = lax.dynamic_index_in_dim(kept, y, 0, False)
        for k in (2, 1, 3):
            piece = lax.dynamic_index_in_dim(kept, (y + k) % ny, 0, False).astype(LOW)
            total = total + shift(piece, Y, ny, k).astype(F32)

    with jax.named_scope("screen"):
        place = z * width + lax.axis_index(PLANE) * count
        unit = (lax.iota(jnp.int32, count)[:, None] + place) == lax.iota(jnp.int32, panel)[None, :]
        screened = jnp.dot(
            unit.astype(F32) + total, block_inverse, precision=lax.Precision.HIGH
        )

    with jax.named_scope("gather_y"):
        low = screened.astype(LOW)
        steps = (0, 2, 1, 3)
        gathered = jnp.concatenate([low] + [shift(low, Y, ny, k) for k in steps[1:]], axis=0)
        by_y = factors.reshape(ny, count, -1)
        ordered = jnp.concatenate(
            [lax.dynamic_index_in_dim(by_y, (y - k) % ny, 0, False) for k in steps], axis=0
        )

    with jax.named_scope("sigma"):
        panels = jnp.concatenate(early + late, axis=0)
        products = lax.dot_general(
            gathered, panels, (((1,), (1,)), ((), ())), preferred_element_type=F32
        )
        local = -jnp.sum(products * ordered.astype(F32), axis=0).reshape(2 * nx, own)
        a, b, c = local[2:4], local[4:6], local[6:]
        offsets = [
            local[:2],
            jnp.where(is0, b, a),
            jnp.where(is0, c, c[::-1]),
            jnp.where(is0, a, b),
        ]
        to = (lax.iota(jnp.int32, nx) - x) % nx
        by_x = sum(
            jnp.where((to == k)[:, None, None], offsets[k][None], 0.0) for k in range(nx)
        )
        copies = jnp.broadcast_to(by_x[:, :, None], (nx, 2, nz, own)).reshape(-1, own)
        terms = lax.all_to_all(copies, (X, CORE, Z), 0, 0, tiled=True)
        sigma = jnp.sum(terms, axis=0)
    return sigma, screened[None]


def solution(mesh):
    split = Mesh(mesh.devices.reshape(2, 4, 2, 2, 8), ("grp", "x", "ylo", "core", "col"))
    return jax.shard_map(
        body,
        mesh=split,
        in_specs=(P(PLANE, Z), P(PLANE), P()),
        out_specs=(P(PLANE), P(Z, PLANE, None)),
        check_vma=False,
    )
```

```python
import jax
import jax.numpy as jnp
from jax import lax
from jax.sharding import Mesh, PartitionSpec as P

X, Y, Z, CORE = "x", ("grp", "ylo"), "col", "core"
PLANE = ("grp", "x", "ylo", "core")
LOW, F32 = jnp.bfloat16, jnp.float32
def shift(value, axis, size, step):
    return lax.ppermute(value, axis, [(i, (i + step) % size) for i in range(size)])


def along_z(value, *pairs):
    return lax.ppermute(value, Z, pairs)


def swap(value):
    return lax.ppermute(value, CORE, [(0, 1), (1, 0)])


def parts_of(value):
    out = []
    for _ in range(3):
        part = lax.reduce_precision(value, 8, 7)
        out.append(part.astype(LOW))
        value = value - part
    return out


def body(orbital_b, gaps, block_inverse):
    own, width = orbital_b.shape
    panel = block_inverse.shape[0]
    nx, ny, nz = lax.axis_size(X), lax.axis_size(Y), lax.axis_size(Z)
    x, y, z, core = (lax.axis_index(a) for a in (X, Y, Z, CORE))
    count = width // lax.axis_size(PLANE)
    steps = (0, 2, 1, 3)

    with jax.named_scope("panel_z"):
        piece = orbital_b[:, :panel]
        far_a = along_z(piece, (0, 3))
        far_b = along_z(piece, (0, 6))
        near_a = along_z(piece, (0, 1))
        near_b = along_z(piece, (0, 7))

    with jax.named_scope("blocks"):
        weight = 2.0 * gaps / (gaps * gaps + 1.0)
        rows = orbital_b.T.reshape(2, nx, 2, 2, count, own)
        extra = jnp.concatenate(
            [jnp.stack(parts_of(weight)), jnp.zeros((13, own), LOW)], axis=0
        )
        mine = lax.dynamic_index_in_dim(rows, core, 3, False).reshape(-1, own)
        mine = jnp.concatenate([mine, extra], axis=0)
        sent = lax.dynamic_index_in_dim(rows, 1 - core, 3, False).reshape(-1, own)
        sent = jnp.concatenate([sent, extra], axis=0)
        mine, sent, far_a, far_b = lax.optimization_barrier((mine, sent, far_a, far_b))

    with jax.named_scope("panel_z"):
        next_a = along_z(far_a, (3, 4))
        next_b = along_z(far_b, (6, 5))
        next_c = along_z(far_a, (3, 2))
    with jax.named_scope("blocks"):
        pair = jnp.concatenate([mine, swap(sent)], axis=1)
        blocks = pair[:-16].reshape(2, nx, 2 * count, 2 * own)

        def rows_of(i):
            block = lax.dynamic_index_in_dim(blocks, i, 1, False).reshape(-1, 2 * own)
            return jnp.concatenate([block, pair[-16:]], axis=0)

        factors = jnp.concatenate(
            [rows_of(x)] + [shift(rows_of((x + k) % nx), X, nx, k) for k in steps[1:]], axis=1
        )
        weight = jnp.sum(factors[-16:-13].astype(F32), axis=0)
        factors = factors[:-16]

    with jax.named_scope("panel_z"):
        held = jnp.where(z == 3, far_a, jnp.where(z == 6, far_b, piece))
        held = jnp.where(z == 1, near_a, jnp.where(z == 7, near_b, held))
        held = jnp.where(z == 4, next_a, jnp.where(z == 5, next_b, jnp.where(z == 2, next_c, held)))

    with jax.named_scope("panel_x"):
        got = [held] + [shift(held, X, nx, k) for k in steps[1:]]
        panels = [part for one in got for part in (one, swap(one))]

    with jax.named_scope("response"):
        part = 0.0
        half = len(panels) // 2
        for group in (slice(0, half), slice(half, None)):
            block = jnp.concatenate(panels[group], axis=0)
            columns = slice(group.start * own, (group.stop or 2 * half) * own)
            weighted = (weight[columns, None] * block.astype(F32)).astype(LOW)
            part = part + jnp.dot(factors[:, columns], weighted, preferred_element_type=F32)

    with jax.named_scope("sum_y"):
        kept = part.reshape(ny, count, panel)
        total = lax.dynamic_index_in_dim(kept, y, 0, False)
        for k in (2, 1, 3):
            piece = lax.dynamic_index_in_dim(kept, (y + k) % ny, 0, False).astype(LOW)
            total = total + shift(piece, Y, ny, k).astype(F32)

    with jax.named_scope("screen"):
        place = z * width + lax.axis_index(PLANE) * count
        unit = (lax.iota(jnp.int32, count)[:, None] + place) == lax.iota(jnp.int32, panel)[None, :]
        screened = jnp.dot(
            unit.astype(F32) + total, block_inverse, precision=lax.Precision.HIGH
        )

    with jax.named_scope("gather_y"):
        low = screened.astype(LOW)
        gathered = jnp.concatenate([low] + [shift(low, Y, ny, k) for k in steps[1:]], axis=0)
        by_y = factors.reshape(ny, count, -1)
        ordered = jnp.concatenate(
            [lax.dynamic_index_in_dim(by_y, (y - k) % ny, 0, False) for k in steps], axis=0
        )

    with jax.named_scope("sigma"):
        block = jnp.concatenate(panels, axis=0)
        products = lax.dot_general(
            gathered, block, (((1,), (1,)), ((), ())), preferred_element_type=F32
        )
        local = -jnp.sum(products * ordered.astype(F32), axis=0).reshape(nx, 2, own)
        local = local[:, 0] + swap(local[:, 1])
        back = (x - lax.iota(jnp.int32, nx)) % nx
        by_x = sum(
            jnp.where((back == k)[:, None], local[i][None], 0.0) for i, k in enumerate(steps)
        )
        copies = jnp.broadcast_to(by_x[:, None], (nx, nz, own)).reshape(-1, own)
        terms = lax.all_to_all(copies, (X, Z), 0, 0, tiled=True)
        sigma = jnp.sum(terms, axis=0)
    return sigma, screened[None]


def solution(mesh):
    split = Mesh(mesh.devices.reshape(2, 4, 2, 2, 8), ("grp", "x", "ylo", "core", "col"))
    return jax.shard_map(
        body,
        mesh=split,
        in_specs=(P(PLANE, Z), P(PLANE), P()),
        out_specs=(P(PLANE), P(Z, PLANE, None)),
        check_vma=False,
    )
```

```python
import jax
import jax.numpy as jnp
from jax import lax
from jax.sharding import Mesh, PartitionSpec as P

X, Y, Z, CORE = "x", ("grp", "ylo"), "col", "core"
PLANE = ("grp", "x", "ylo", "core")
LOW, F32 = jnp.bfloat16, jnp.float32
def shift(value, axis, size, step):
    return lax.ppermute(value, axis, [(i, (i + step) % size) for i in range(size)])


def along_z(value, *pairs):
    return lax.ppermute(value, Z, pairs)


def swap(value):
    return lax.ppermute(value, CORE, [(0, 1), (1, 0)])


def parts_of(value):
    out = []
    for _ in range(3):
        part = lax.reduce_precision(value, 8, 7)
        out.append(part.astype(LOW))
        value = value - part
    return out


def two_parts(value):
    high = lax.reduce_precision(value, 8, 7)
    return high.astype(LOW), (value - high).astype(LOW)


def body(orbital_b, gaps, block_inverse):
    own, width = orbital_b.shape
    panel = block_inverse.shape[0]
    nx, ny, nz = lax.axis_size(X), lax.axis_size(Y), lax.axis_size(Z)
    x, y, z, core = (lax.axis_index(a) for a in (X, Y, Z, CORE))
    count = width // lax.axis_size(PLANE)
    steps = (0, 2, 1, 3)

    with jax.named_scope("panel_z"):
        piece = orbital_b[:, :panel]
        far_b = along_z(piece, (0, 6))
        far_a = along_z(piece, (0, 3))

    with jax.named_scope("blocks"):
        weight = 2.0 * gaps / (gaps * gaps + 1.0)
        rows = orbital_b.T.reshape(2, nx, 2, 2, count, own)
        extra = jnp.concatenate(
            [jnp.stack(parts_of(weight)), jnp.zeros((13, own), LOW)], axis=0
        )
        mine = lax.dynamic_index_in_dim(rows, core, 3, False).reshape(-1, own)
        mine = jnp.concatenate([mine, extra], axis=0)
        sent = lax.dynamic_index_in_dim(rows, 1 - core, 3, False).reshape(-1, own)
        sent = jnp.concatenate([sent, extra], axis=0)
        mine, sent, far_a, far_b = lax.optimization_barrier((mine, sent, far_a, far_b))

    with jax.named_scope("panel_z"):
        held = jnp.where(z == 3, far_a, jnp.where(z == 6, far_b, piece))
        near_a = along_z(held, (0, 1), (3, 4), (6, 5))
        near_b = along_z(held, (0, 7), (3, 2))
        inv_high, inv_rest = two_parts(block_inverse)
        near_a, near_b, inv_high, inv_rest = lax.optimization_barrier(
            (near_a, near_b, inv_high, inv_rest)
        )
        held = jnp.where((z == 1) | (z == 4) | (z == 5), near_a, held)
        held = jnp.where((z == 7) | (z == 2), near_b, held)

    with jax.named_scope("blocks"):
        pair = jnp.concatenate([mine, swap(sent)], axis=1)
        blocks = pair[:-16].reshape(2, nx, 2 * count, 2 * own)

        def rows_of(i):
            block = lax.dynamic_index_in_dim(blocks, i, 1, False).reshape(-1, 2 * own)
            return jnp.concatenate([block, pair[-16:]], axis=0)

        factors = jnp.concatenate(
            [rows_of(x)] + [shift(rows_of((x + k) % nx), X, nx, k) for k in steps[1:]], axis=1
        )
        weight = jnp.sum(factors[-16:-13].astype(F32), axis=0)
        factors = factors[:-16]

    with jax.named_scope("panel_x"):
        got = [held] + [shift(held, X, nx, k) for k in steps[1:]]
        panels = [part for one in got for part in (one, swap(one))]

    with jax.named_scope("response"):
        part = 0.0
        half = len(panels) // 2
        for group in (slice(0, half), slice(half, None)):
            block = jnp.concatenate(panels[group], axis=0)
            columns = slice(group.start * own, (group.stop or 2 * half) * own)
            weighted = (weight[columns, None] * block.astype(F32)).astype(LOW)
            part = part + jnp.dot(factors[:, columns], weighted, preferred_element_type=F32)

    with jax.named_scope("sum_y"):
        kept = part.reshape(ny, count, panel)
        total = lax.dynamic_index_in_dim(kept, y, 0, False)
        for k in (2, 1, 3):
            piece = lax.dynamic_index_in_dim(kept, (y + k) % ny, 0, False).astype(LOW)
            total = total + shift(piece, Y, ny, k).astype(F32)

    with jax.named_scope("screen"):
        place = z * width + lax.axis_index(PLANE) * count
        unit = (lax.iota(jnp.int32, count)[:, None] + place) == lax.iota(jnp.int32, panel)[None, :]
        total = unit.astype(F32) + total
        high, rest = two_parts(total)
        screened = jnp.dot(
            jnp.concatenate([high, rest], axis=0), inv_high, preferred_element_type=F32
        )
        screened = screened[:count] + screened[count:]
        screened = screened + jnp.dot(high, inv_rest, preferred_element_type=F32)

    with jax.named_scope("gather_y"):
        low = screened.astype(LOW)
        gathered = jnp.concatenate([low] + [shift(low, Y, ny, k) for k in steps[1:]], axis=0)
        by_y = factors.reshape(ny, count, -1)
        ordered = jnp.concatenate(
            [lax.dynamic_index_in_dim(by_y, (y - k) % ny, 0, False) for k in steps], axis=0
        )

    with jax.named_scope("sigma"):
        block = jnp.concatenate(panels, axis=0)
        products = lax.dot_general(
            gathered, block, (((1,), (1,)), ((), ())), preferred_element_type=F32
        )
        local = -jnp.sum(products * ordered.astype(F32), axis=0).reshape(nx, 2, own)
        local = local[:, 0] + swap(local[:, 1])
        back = (x - lax.iota(jnp.int32, nx)) % nx
        by_x = sum(
            jnp.where((back == k)[:, None], local[i][None], 0.0) for i, k in enumerate(steps)
        )
        copies = jnp.broadcast_to(by_x[:, None], (nx, nz, own)).reshape(-1, own)
        terms = lax.all_to_all(copies, (X, Z), 0, 0, tiled=True)
        sigma = jnp.sum(terms, axis=0)
    return sigma, screened[None]


def solution(mesh):
    split = Mesh(mesh.devices.reshape(2, 4, 2, 2, 8), ("grp", "x", "ylo", "core", "col"))
    return jax.shard_map(
        body,
        mesh=split,
        in_specs=(P(PLANE, Z), P(PLANE), P()),
        out_specs=(P(PLANE), P(Z, PLANE, None)),
        check_vma=False,
    )
```

```python
import jax
import jax.numpy as jnp
from jax import lax
from jax.sharding import Mesh, PartitionSpec as P

X, Y, Z, CORE = "x", ("grp", "ylo"), "col", "core"
PLANE = ("grp", "x", "ylo", "core")
LOW, F32 = jnp.bfloat16, jnp.float32
def shift(value, axis, size, step):
    return lax.ppermute(value, axis, [(i, (i + step) % size) for i in range(size)])


def along_z(value, *pairs):
    return lax.ppermute(value, Z, pairs)


def swap(value):
    return lax.ppermute(value, CORE, [(0, 1), (1, 0)])


def parts_of(value):
    out = []
    for _ in range(3):
        part = lax.reduce_precision(value, 8, 7)
        out.append(part.astype(LOW))
        value = value - part
    return out


def two_parts(value):
    high = lax.reduce_precision(value, 8, 7)
    return high.astype(LOW), (value - high).astype(LOW)


def body(orbital_b, gaps, block_inverse):
    own, width = orbital_b.shape
    panel = block_inverse.shape[0]
    nx, ny, nz = lax.axis_size(X), lax.axis_size(Y), lax.axis_size(Z)
    x, y, z, core = (lax.axis_index(a) for a in (X, Y, Z, CORE))
    count = width // lax.axis_size(PLANE)
    steps = (0, 2, 1, 3)

    with jax.named_scope("panel_z"):
        piece = orbital_b[:, :panel]
        far_a = along_z(piece, (0, 3))
        far_b = along_z(piece, (0, 6))

    with jax.named_scope("blocks"):
        weight = 2.0 * gaps / (gaps * gaps + 1.0)
        extra = jnp.concatenate(
            [jnp.stack(parts_of(weight)), jnp.zeros((13, own), LOW)], axis=0
        )
        blocks = orbital_b.T.reshape(2, nx, -1, own)

        def rows_of(i):
            block = lax.dynamic_index_in_dim(blocks, i, 1, False).reshape(-1, own)
            return jnp.concatenate([block, extra], axis=0)

        rows = [rows_of((x + k) % nx) for k in steps]
        factors = [rows[0]] + [shift(row, X, nx, k) for row, k in zip(rows[1:], steps[1:])]

    with jax.named_scope("panel_z"):
        far_a, far_b, block_inverse, *_ = lax.optimization_barrier(
            (far_a, far_b, block_inverse, *rows)
        )
        held = jnp.where(z == 3, far_a, jnp.where(z == 6, far_b, piece))
        near_a = along_z(held, (0, 1), (3, 4), (6, 5))
        near_b = along_z(held, (0, 7), (3, 2))
        inv_high, inv_rest = two_parts(block_inverse)
        near_a, near_b, inv_high, inv_rest, *factors = lax.optimization_barrier(
            (near_a, near_b, inv_high, inv_rest, *factors)
        )
        held = jnp.where((z == 1) | (z == 4) | (z == 5), near_a, held)
        held = jnp.where((z == 7) | (z == 2), near_b, held)

    with jax.named_scope("panel_x"):
        panels = [held] + [shift(held, X, nx, k) for k in steps[1:]]
        panels = jnp.concatenate(panels, axis=0)

    with jax.named_scope("response"):
        factors = jnp.concatenate(factors, axis=1)
        weight = jnp.sum(factors[-16:-13].astype(F32), axis=0)
        factors = factors[:-16]
        weighted = (weight[:, None] * panels.astype(F32)).astype(LOW)
        part = jnp.dot(factors, weighted, preferred_element_type=F32)

    with jax.named_scope("sum_core"):
        part = part.reshape(ny, 2, count, panel)
        sent = lax.dynamic_index_in_dim(part, 1 - core, 1, False)
        kept = lax.dynamic_index_in_dim(part, core, 1, False) + swap(sent)

    with jax.named_scope("sum_y"):
        total = lax.dynamic_index_in_dim(kept, y, 0, False)
        for k in (2, 1, 3):
            piece = lax.dynamic_index_in_dim(kept, (y + k) % ny, 0, False).astype(LOW)
            total = total + shift(piece, Y, ny, k).astype(F32)

    with jax.named_scope("screen"):
        place = z * width + lax.axis_index(PLANE) * count
        unit = (lax.iota(jnp.int32, count)[:, None] + place) == lax.iota(jnp.int32, panel)[None, :]
        total = unit.astype(F32) + total
        high, rest = two_parts(total)
        screened = jnp.dot(
            jnp.concatenate([high, rest], axis=0), inv_high, preferred_element_type=F32
        )
        screened = screened[:count] + screened[count:]
        screened = screened + jnp.dot(high, inv_rest, preferred_element_type=F32)

    with jax.named_scope("gather_y"):
        low = screened.astype(LOW)
        gathered = jnp.concatenate([low] + [shift(low, Y, ny, k) for k in steps[1:]], axis=0)
        gathered = jnp.concatenate([gathered, swap(gathered)], axis=0)
        by_y = factors.reshape(ny, 2, count, -1)
        ordered = jnp.concatenate(
            [
                lax.dynamic_slice(by_y, ((y - k) % ny, c, 0, 0), (1, 1, count, nx * own))
                for c in (core, 1 - core)
                for k in steps
            ]
        ).reshape(-1, nx * own)

    with jax.named_scope("sigma"):
        products = lax.dot_general(
            gathered, panels, (((1,), (1,)), ((), ())), preferred_element_type=F32
        )
        local = -jnp.sum(products * ordered.astype(F32), axis=0).reshape(nx, own)
        back = (x - lax.iota(jnp.int32, nx)) % nx
        by_x = sum(
            jnp.where((back == k)[:, None], local[i][None], 0.0) for i, k in enumerate(steps)
        )
        copies = jnp.broadcast_to(by_x[:, None], (nx, nz, own)).reshape(-1, own)
        terms = lax.all_to_all(copies, (X, Z), 0, 0, tiled=True)
        sigma = jnp.sum(terms, axis=0)
    return sigma, screened[None]


def solution(mesh):
    split = Mesh(mesh.devices.reshape(2, 4, 2, 2, 8), ("grp", "x", "ylo", "core", "col"))
    return jax.shard_map(
        body,
        mesh=split,
        in_specs=(P(PLANE, Z), P(PLANE), P()),
        out_specs=(P(PLANE), P(Z, PLANE, None)),
        check_vma=False,
    )
```

```python
import jax
import jax.numpy as jnp
from jax import lax
from jax.sharding import Mesh, PartitionSpec as P

X, Y, Z, CORE = "x", ("grp", "ylo"), "col", "core"
PLANE = ("grp", "x", "ylo", "core")
LOW, F32 = jnp.bfloat16, jnp.float32
def shift(value, axis, size, step):
    return lax.ppermute(value, axis, [(i, (i + step) % size) for i in range(size)])


def along_z(value, *pairs):
    return lax.ppermute(value, Z, pairs)


def from_zero(value, *targets):
    return lax.ppermute(value, (CORE, Z), [(c * 8, c * 8 + z) for c, z in enumerate(targets)])


def turn(value, size, step):
    pairs = []
    for x in range(size):
        pairs += [(x * 2, (x + step) % size * 2), (x * 2 + 1, (x - step) % size * 2 + 1)]
    return lax.ppermute(value, (X, CORE), pairs)


def swap(value):
    return lax.ppermute(value, CORE, [(0, 1), (1, 0)])


def parts_of(value):
    out = []
    for _ in range(3):
        part = lax.reduce_precision(value, 8, 7)
        out.append(part.astype(LOW))
        value = value - part
    return out


def two_parts(value):
    high = lax.reduce_precision(value, 8, 7)
    return high.astype(LOW), (value - high).astype(LOW)


def body(orbital_b, gaps, block_inverse):
    own, width = orbital_b.shape
    panel = block_inverse.shape[0]
    nx, ny, nz = lax.axis_size(X), lax.axis_size(Y), lax.axis_size(Z)
    x, y, z, core = (lax.axis_index(a) for a in (X, Y, Z, CORE))
    count = width // lax.axis_size(PLANE)
    steps = (0, 2, 1, 3)
    way = 1 - 2 * core

    with jax.named_scope("panel_z"):
        piece = orbital_b[:, :panel]
        far_a = from_zero(piece, 3, 6)
        far_b = from_zero(piece, 6, 3)
        first = along_z(piece, (0, 1))

    with jax.named_scope("blocks"):
        weight = 2.0 * gaps / (gaps * gaps + 1.0)
        extra = jnp.concatenate(
            [jnp.stack(parts_of(weight)), jnp.zeros((13, own), LOW)], axis=0
        )
        blocks = orbital_b.T.reshape(2, nx, -1, own)

        def rows_of(i):
            block = lax.dynamic_index_in_dim(blocks, i, 1, False).reshape(-1, own)
            return jnp.concatenate([block, extra], axis=0)

        rows = [rows_of((x + way * k) % nx) for k in steps]
        factors = [rows[0]] + [turn(row, nx, k) for row, k in zip(rows[1:], steps[1:])]

    with jax.named_scope("panel_z"):
        far_a, far_b, block_inverse, *_ = lax.optimization_barrier(
            (far_a, far_b, block_inverse, *rows)
        )
        held = jnp.where(z == jnp.where(core == 0, 3, 6), far_a, piece)
        held = jnp.where(z == jnp.where(core == 0, 6, 3), far_b, held)
        near_a = along_z(held, (3, 4), (6, 5))
        near_b = along_z(held, (3, 2), (6, 7))
        inv_high, inv_rest = two_parts(block_inverse)
        near_a, near_b, inv_high, inv_rest, *factors = lax.optimization_barrier(
            (near_a, near_b, inv_high, inv_rest, *factors)
        )
        held = jnp.where(z == 1, first, held)
        held = jnp.where((z == 4) | (z == 5), near_a, held)
        held = jnp.where((z == 7) | (z == 2), near_b, held)

    with jax.named_scope("panel_x"):
        ahead = turn(held, nx, 1)
        behind = turn(held, nx, 3)
        panels = jnp.concatenate([held, turn(ahead, nx, 1), ahead, behind], axis=0)

    with jax.named_scope("response"):
        factors = jnp.concatenate(factors, axis=1)
        weight = jnp.sum(factors[-16:-13].astype(F32), axis=0)
        factors = factors[:-16]
        weighted = (weight[:, None] * panels.astype(F32)).astype(LOW)
        part = jnp.dot(factors, weighted, preferred_element_type=F32)

    with jax.named_scope("sum_core"):
        part = part.reshape(ny, 2, count, panel)
        sent = lax.dynamic_index_in_dim(part, 1 - core, 1, False)
        kept = lax.dynamic_index_in_dim(part, core, 1, False) + swap(sent)

    with jax.named_scope("sum_y"):
        total = lax.dynamic_index_in_dim(kept, y, 0, False)
        for k in (2, 1, 3):
            piece = lax.dynamic_index_in_dim(kept, (y + k) % ny, 0, False).astype(LOW)
            total = total + shift(piece, Y, ny, k).astype(F32)

    with jax.named_scope("screen"):
        place = z * width + lax.axis_index(PLANE) * count
        unit = (lax.iota(jnp.int32, count)[:, None] + place) == lax.iota(jnp.int32, panel)[None, :]
        total = unit.astype(F32) + total
        high, rest = two_parts(total)
        screened = jnp.dot(
            jnp.concatenate([high, rest], axis=0), inv_high, preferred_element_type=F32
        )
        screened = screened[:count] + screened[count:]
        screened = screened + jnp.dot(high, inv_rest, preferred_element_type=F32)

    with jax.named_scope("gather_y"):
        low = screened.astype(LOW)
        gathered = jnp.concatenate([low] + [shift(low, Y, ny, k) for k in steps[1:]], axis=0)
        gathered = jnp.concatenate([gathered, swap(gathered)], axis=0)
        by_y = factors.reshape(ny, 2, count, -1)
        ordered = jnp.concatenate(
            [
                lax.dynamic_slice(by_y, ((y - k) % ny, c, 0, 0), (1, 1, count, nx * own))
                for c in (core, 1 - core)
                for k in steps
            ]
        ).reshape(-1, nx * own)

    with jax.named_scope("sigma"):
        products = lax.dot_general(
            gathered, panels, (((1,), (1,)), ((), ())), preferred_element_type=F32
        )
        local = -jnp.sum(products * ordered.astype(F32), axis=0).reshape(nx, own)
        back = way * (x - lax.iota(jnp.int32, nx)) % nx
        by_x = sum(
            jnp.where((back == k)[:, None], local[i][None], 0.0) for i, k in enumerate(steps)
        )
        copies = jnp.broadcast_to(by_x[:, None], (nx, nz, own)).reshape(-1, own)
        terms = lax.all_to_all(copies, (X, Z), 0, 0, tiled=True)
        sigma = jnp.sum(terms, axis=0)
    return sigma, screened[None]


def solution(mesh):
    split = Mesh(mesh.devices.reshape(2, 4, 2, 2, 8), ("grp", "x", "ylo", "core", "col"))
    return jax.shard_map(
        body,
        mesh=split,
        in_specs=(P(PLANE, Z), P(PLANE), P()),
        out_specs=(P(PLANE), P(Z, PLANE, None)),
        check_vma=False,
    )
```

```python
import jax
import jax.numpy as jnp
from jax import lax
from jax.sharding import Mesh, PartitionSpec as P

X, Y, Z, CORE = "x", ("grp", "ylo"), "col", "core"
PLANE = ("grp", "x", "ylo", "core")
LOW, F32 = jnp.bfloat16, jnp.float32
def shift(value, axis, size, step):
    return lax.ppermute(value, axis, [(i, (i + step) % size) for i in range(size)])


def along_z(value, *pairs):
    return lax.ppermute(value, Z, pairs)


def along_x(value, size, step, columns):
    pairs = [(i * 8 + z, (i + step) % size * 8 + z) for i in range(size) for z in columns]
    return lax.ppermute(value, (X, Z), pairs)


def swap(value):
    return lax.ppermute(value, CORE, [(0, 1), (1, 0)])


def parts_of(value):
    out = []
    for _ in range(3):
        part = lax.reduce_precision(value, 8, 7)
        out.append(part.astype(LOW))
        value = value - part
    return out


def two_parts(value):
    high = lax.reduce_precision(value, 8, 7)
    return high.astype(LOW), (value - high).astype(LOW)


def body(orbital_b, gaps, block_inverse):
    own, width = orbital_b.shape
    panel = block_inverse.shape[0]
    nx, ny, nz = lax.axis_size(X), lax.axis_size(Y), lax.axis_size(Z)
    x, y, z, core = (lax.axis_index(a) for a in (X, Y, Z, CORE))
    count = width // lax.axis_size(PLANE)
    steps = (0, 2, 1, 3)

    with jax.named_scope("panel_z"):
        piece = orbital_b[:, :panel]
        far_a = along_z(piece, (0, 3))
        far_b = along_z(piece, (0, 6))

    with jax.named_scope("blocks"):
        weight = 2.0 * gaps / (gaps * gaps + 1.0)
        extra = jnp.concatenate(
            [jnp.stack(parts_of(weight)), jnp.zeros((13, own), LOW)], axis=0
        )
        blocks = orbital_b.T.reshape(2, nx, -1, own)

        def rows_of(i):
            block = lax.dynamic_index_in_dim(blocks, i, 1, False).reshape(-1, own)
            return jnp.concatenate([block, extra], axis=0)

        rows = [rows_of((x + k) % nx) for k in steps]
        factors = [rows[0]] + [shift(row, X, nx, k) for row, k in zip(rows[1:], steps[1:])]

    with jax.named_scope("panel_z"):
        far_a, far_b, block_inverse, *_ = lax.optimization_barrier(
            (far_a, far_b, block_inverse, *rows)
        )
        held = jnp.where(z == 3, far_a, jnp.where(z == 6, far_b, piece))
        near_a = along_z(held, (0, 1), (3, 4), (6, 5))
        near_b = along_z(held, (0, 7), (3, 2))
        far_x = along_x(held, nx, 2, (0, 3, 6))
        far_near_a = along_z(far_x, (0, 1), (3, 4), (6, 5))
        far_near_b = along_z(far_x, (0, 7), (3, 2))
        inv_high, inv_rest = two_parts(block_inverse)
        near_a, near_b, inv_high, inv_rest, _, *factors = lax.optimization_barrier(
            (near_a, near_b, inv_high, inv_rest, far_x, *factors)
        )
        from_a, from_b = (z == 1) | (z == 4) | (z == 5), (z == 7) | (z == 2)
        held = jnp.where(from_a, near_a, jnp.where(from_b, near_b, held))

    with jax.named_scope("panel_x"):
        right, left = shift(held, X, nx, 1), shift(held, X, nx, 3)
        far_x = jnp.where(from_a, far_near_a, jnp.where(from_b, far_near_b, far_x))
        panels = jnp.concatenate([held, far_x, right, left], axis=0)

    with jax.named_scope("response"):
        factors = jnp.concatenate(factors, axis=1)
        weight = jnp.sum(factors[-16:-13].astype(F32), axis=0)
        factors = factors[:-16]
        weighted = (weight[:, None] * panels.astype(F32)).astype(LOW)
        part = jnp.dot(factors, weighted, preferred_element_type=F32)

    with jax.named_scope("sum_core"):
        part = part.reshape(ny, 2, count, panel)
        sent = lax.dynamic_index_in_dim(part, 1 - core, 1, False)
        kept = lax.dynamic_index_in_dim(part, core, 1, False) + swap(sent)

    with jax.named_scope("sum_y"):
        total = lax.dynamic_index_in_dim(kept, y, 0, False)
        for k in (2, 1, 3):
            piece = lax.dynamic_index_in_dim(kept, (y + k) % ny, 0, False).astype(LOW)
            total = total + shift(piece, Y, ny, k).astype(F32)

    with jax.named_scope("screen"):
        place = z * width + lax.axis_index(PLANE) * count
        unit = (lax.iota(jnp.int32, count)[:, None] + place) == lax.iota(jnp.int32, panel)[None, :]
        total = unit.astype(F32) + total
        high, rest = two_parts(total)
        screened = jnp.dot(
            jnp.concatenate([high, rest], axis=0), inv_high, preferred_element_type=F32
        )
        screened = screened[:count] + screened[count:]
        screened = screened + jnp.dot(high, inv_rest, preferred_element_type=F32)

    with jax.named_scope("gather_y"):
        low = screened.astype(LOW)
        gathered = jnp.concatenate([low] + [shift(low, Y, ny, k) for k in steps[1:]], axis=0)
        gathered = jnp.concatenate([gathered, swap(gathered)], axis=0)
        by_y = factors.reshape(ny, 2, count, -1)
        ordered = jnp.concatenate(
            [
                lax.dynamic_slice(by_y, ((y - k) % ny, c, 0, 0), (1, 1, count, nx * own))
                for c in (core, 1 - core)
                for k in steps
            ]
        ).reshape(-1, nx * own)

    with jax.named_scope("sigma"):
        products = lax.dot_general(
            gathered, panels, (((1,), (1,)), ((), ())), preferred_element_type=F32
        )
        local = -jnp.sum(products * ordered.astype(F32), axis=0).reshape(nx, own)
        back = (x - lax.iota(jnp.int32, nx)) % nx
        by_x = sum(
            jnp.where((back == k)[:, None], local[i][None], 0.0) for i, k in enumerate(steps)
        )
        copies = jnp.broadcast_to(by_x[:, None], (nx, nz, own)).reshape(-1, own)
        terms = lax.all_to_all(copies, (X, Z), 0, 0, tiled=True)
        sigma = jnp.sum(terms, axis=0)
    return sigma, screened[None]


def solution(mesh):
    split = Mesh(mesh.devices.reshape(2, 4, 2, 2, 8), ("grp", "x", "ylo", "core", "col"))
    return jax.shard_map(
        body,
        mesh=split,
        in_specs=(P(PLANE, Z), P(PLANE), P()),
        out_specs=(P(PLANE), P(Z, PLANE, None)),
        check_vma=False,
    )
```

```python
import jax
import jax.numpy as jnp
from jax import lax
from jax.sharding import Mesh, PartitionSpec as P

X, Y, Z, CORE = "x", ("grp", "ylo"), "col", "core"
PLANE = ("grp", "x", "ylo", "core")
LOW, F32 = jnp.bfloat16, jnp.float32
def shift(value, axis, size, step):
    return lax.ppermute(value, axis, [(i, (i + step) % size) for i in range(size)])


def along_z(value, *pairs):
    return lax.ppermute(value, Z, pairs)


def along_x(value, size, step, columns):
    pairs = [(i * 8 + z, (i + step) % size * 8 + z) for i in range(size) for z in columns]
    return lax.ppermute(value, (X, Z), pairs)


def swap(value):
    return lax.ppermute(value, CORE, [(0, 1), (1, 0)])


def parts_of(value):
    out = []
    for _ in range(3):
        part = lax.reduce_precision(value, 8, 7)
        out.append(part.astype(LOW))
        value = value - part
    return out


def two_parts(value):
    high = lax.reduce_precision(value, 8, 7)
    return high.astype(LOW), (value - high).astype(LOW)


def body(orbital_b, gaps, block_inverse):
    own, width = orbital_b.shape
    panel = block_inverse.shape[0]
    nx, ny, nz = lax.axis_size(X), lax.axis_size(Y), lax.axis_size(Z)
    x, y, z, core = (lax.axis_index(a) for a in (X, Y, Z, CORE))
    count = width // lax.axis_size(PLANE)
    quarter = panel // nx
    steps = (0, 2, 1, 3)

    def by_place(values):
        return [
            sum(
                jnp.where((x - k) % nx == q, value, jnp.zeros_like(value))
                for k, value in zip(steps, values)
            )
            for q in range(nx)
        ]

    with jax.named_scope("quarters"):
        def quarter_of(i):
            return lax.dynamic_slice(orbital_b, (0, i * quarter), (own, quarter))

        got = [quarter_of(x)]
        got += [along_x(quarter_of((x + k) % nx), nx, k, (0,)) for k in steps[1:]]
        piece = jnp.concatenate(got, axis=0)

    with jax.named_scope("panel_z"):
        far_a = along_z(piece, (0, 3))
        far_b = along_z(piece, (0, 6))

    with jax.named_scope("blocks"):
        weight = 2.0 * gaps / (gaps * gaps + 1.0)
        rows, piece = lax.optimization_barrier((orbital_b, piece))
        rows = jnp.concatenate(
            [rows.T, jnp.stack(parts_of(weight)), jnp.zeros((13, own), LOW)], axis=0
        )
        factors = [rows] + [shift(rows, X, nx, k) for k in steps[1:]]

    with jax.named_scope("panel_z"):
        far_a, far_b, block_inverse, _ = lax.optimization_barrier(
            (far_a, far_b, block_inverse, rows)
        )
        held = jnp.where(z == 3, far_a, jnp.where(z == 6, far_b, piece))
        near_a = along_z(held, (0, 1), (3, 4), (6, 5))
        near_b = along_z(held, (0, 7), (3, 2))
        inv_high, inv_rest = two_parts(block_inverse)
        near_a, near_b, inv_high, inv_rest = lax.optimization_barrier(
            (near_a, near_b, inv_high, inv_rest)
        )
        held = jnp.where((z == 1) | (z == 4) | (z == 5), near_a, held)
        held = jnp.where((z == 7) | (z == 2), near_b, held)

    with jax.named_scope("response"):
        factors = jnp.concatenate(factors, axis=1)
        weight = jnp.sum(factors[width : width + 3].astype(F32), axis=0)
        factors = factors[:width]
        weighted = (weight[:, None] * held.astype(F32)).astype(LOW)
        part = jnp.dot(factors, weighted, preferred_element_type=F32)

    with jax.named_scope("sum_core"):
        part = part.reshape(2, nx, 2, 2, count, quarter)
        sent = lax.dynamic_index_in_dim(part, 1 - core, 3, False)
        kept = lax.dynamic_index_in_dim(part, core, 3, False) + swap(sent)

    with jax.named_scope("sum_y"):

        def rows_at(i):
            block = lax.dynamic_slice(
                kept, (i // 2, 0, i % 2, 0, 0), (1, nx, 1, count, quarter)
            )
            return block.reshape(nx * count, quarter)

        total = rows_at(y)
        for k in steps[1:]:
            total = total + shift(rows_at((y + k) % ny).astype(LOW), Y, ny, k).astype(F32)

    with jax.named_scope("exchange_x"):
        total = total.reshape(nx, count, quarter)
        held, total = lax.optimization_barrier((held, total))
        panels = [held] + [shift(held, X, nx, k) for k in steps[1:]]
        own_rows = [lax.dynamic_index_in_dim(total, x, 0, False)]
        for k in steps[1:]:
            own_rows.append(
                shift(lax.dynamic_index_in_dim(total, (x + k) % nx, 0, False), X, nx, k)
            )
        total = jnp.concatenate(by_place(own_rows), axis=1)

    with jax.named_scope("screen"):
        place = z * width + lax.axis_index(PLANE) * count
        unit = (lax.iota(jnp.int32, count)[:, None] + place) == lax.iota(jnp.int32, panel)[None, :]
        total = unit.astype(F32) + total
        high, rest = two_parts(total)
        screened = jnp.dot(
            jnp.concatenate([high, rest], axis=0), inv_high, preferred_element_type=F32
        )
        screened = screened[:count] + screened[count:]
        screened = screened + jnp.dot(high, inv_rest, preferred_element_type=F32)

    with jax.named_scope("gather_y"):
        low = screened.astype(LOW)
        gathered = jnp.concatenate([low] + [shift(low, Y, ny, k) for k in steps[1:]], axis=0)
        gathered, *panels = lax.optimization_barrier((gathered, *panels))
        gathered = jnp.concatenate([gathered, swap(gathered)], axis=0)
        for i, k in enumerate(steps):
            block = panels[i].reshape(nx, own, quarter)
            panels[i] = jnp.concatenate(
                [block[steps.index((m - k) % nx)] for m in steps], axis=0
            )
        panels = jnp.concatenate(by_place(panels), axis=1)


        block = factors.reshape(2, nx, 2, 2, count, nx * own)
        ordered = jnp.concatenate(
            [
                lax.dynamic_slice(
                    block,
                    ((y - k) % ny // 2, x, (y - k) % ny % 2, c, 0, 0),
                    (1, 1, 1, 1, count, nx * own),
                ).reshape(count, nx * own)
                for c in (core, 1 - core)
                for k in steps
            ],
            axis=0,
        )

    with jax.named_scope("sigma"):
        products = lax.dot_general(
            gathered, panels, (((1,), (1,)), ((), ())), preferred_element_type=F32
        )
        local = -jnp.sum(products * ordered.astype(F32), axis=0).reshape(nx, own)
        local = jnp.stack(by_place(list(local)))
        copies = jnp.broadcast_to(local[:, None], (nx, nz, own)).reshape(-1, own)
        terms = lax.all_to_all(copies, (X, Z), 0, 0, tiled=True)
        sigma = jnp.sum(terms, axis=0)
    return sigma, screened[None]


def solution(mesh):
    split = Mesh(mesh.devices.reshape(2, 4, 2, 2, 8), ("grp", "x", "ylo", "core", "col"))
    return jax.shard_map(
        body,
        mesh=split,
        in_specs=(P(PLANE, Z), P(PLANE), P()),
        out_specs=(P(PLANE), P(Z, PLANE, None)),
        check_vma=False,
    )
```

```python
import jax
import jax.numpy as jnp
from jax import lax
from jax.sharding import Mesh, PartitionSpec as P

X, Y, Z, CORE = "x", ("grp", "ylo"), "col", "core"
PLANE = ("grp", "x", "ylo", "core")
LOW, F32 = jnp.bfloat16, jnp.float32
def shift(value, axis, size, step):
    return lax.ppermute(value, axis, [(i, (i + step) % size) for i in range(size)])


def along_z(value, *pairs):
    return lax.ppermute(value, Z, pairs)


def cross(value, size, step, *columns):
    pairs = [(i * 8 + a, (i + step) % size * 8 + b) for i in range(size) for a, b in columns]
    return lax.ppermute(value, (X, Z), pairs)


def swap(value):
    return lax.ppermute(value, CORE, [(0, 1), (1, 0)])


def parts_of(value):
    out = []
    for _ in range(3):
        part = lax.reduce_precision(value, 8, 7)
        out.append(part.astype(LOW))
        value = value - part
    return out


def two_parts(value):
    high = lax.reduce_precision(value, 8, 7)
    return high.astype(LOW), (value - high).astype(LOW)


def body(orbital_b, gaps, block_inverse):
    own, width = orbital_b.shape
    panel = block_inverse.shape[0]
    nx, ny, nz = lax.axis_size(X), lax.axis_size(Y), lax.axis_size(Z)
    x, y, z, core = (lax.axis_index(a) for a in (X, Y, Z, CORE))
    count = width // lax.axis_size(PLANE)
    steps = (0, 2, 1, 3)

    with jax.named_scope("panel_z"):
        piece = orbital_b[:, :panel]
        far_a = along_z(piece, (0, 3))
        far_b = along_z(piece, (0, 6))

    with jax.named_scope("blocks"):
        weight = 2.0 * gaps / (gaps * gaps + 1.0)
        extra = jnp.concatenate(
            [jnp.stack(parts_of(weight)), jnp.zeros((13, own), LOW)], axis=0
        )
        blocks = orbital_b.T.reshape(2, nx, -1, own)

        def rows_of(i):
            block = lax.dynamic_index_in_dim(blocks, i, 1, False).reshape(-1, own)
            return jnp.concatenate([block, extra], axis=0)

        rows = [rows_of((x + k) % nx) for k in steps]
        factors = [rows[0]] + [shift(row, X, nx, k) for row, k in zip(rows[1:], steps[1:])]

    with jax.named_scope("panel_z"):
        far_a, far_b, block_inverse, *_ = lax.optimization_barrier(
            (far_a, far_b, block_inverse, *rows)
        )
        held = jnp.where(z == 3, far_a, jnp.where(z == 6, far_b, piece))
        near_a = along_z(held, (0, 1), (3, 4), (6, 5))
        near_b = along_z(held, (0, 7), (3, 2))
        cross_a = cross(held, nx, 2, (0, 1), (3, 4), (6, 5))
        cross_b = cross(held, nx, 2, (0, 7), (3, 2))
        cross_c = cross(held, nx, 2, (0, 0), (3, 3), (6, 6))
        inv_high, inv_rest = two_parts(block_inverse)
        near_a, near_b, inv_high, inv_rest, *factors = lax.optimization_barrier(
            (near_a, near_b, inv_high, inv_rest, *factors)
        )
        from_a, from_b = (z == 1) | (z == 4) | (z == 5), (z == 7) | (z == 2)
        held = jnp.where(from_a, near_a, jnp.where(from_b, near_b, held))

    with jax.named_scope("panel_x"):
        right, left = shift(held, X, nx, 1), shift(held, X, nx, 3)
        far = jnp.where(from_a, cross_a, jnp.where(from_b, cross_b, cross_c))
        panels = jnp.concatenate([held, far, right, left], axis=0)

    with jax.named_scope("response"):
        factors = jnp.concatenate(factors, axis=1)
        weight = jnp.sum(factors[-16:-13].astype(F32), axis=0)
        factors = factors[:-16]
        weighted = (weight[:, None] * panels.astype(F32)).astype(LOW)
        part = jnp.dot(factors, weighted, preferred_element_type=F32)

    with jax.named_scope("sum_core"):
        part = part.reshape(ny, 2, count, panel)
        sent = lax.dynamic_index_in_dim(part, 1 - core, 1, False)
        kept = lax.dynamic_index_in_dim(part, core, 1, False) + swap(sent)

    with jax.named_scope("sum_y"):
        total = lax.dynamic_index_in_dim(kept, y, 0, False)
        for k in (2, 1, 3):
            piece = lax.dynamic_index_in_dim(kept, (y + k) % ny, 0, False).astype(LOW)
            total = total + shift(piece, Y, ny, k).astype(F32)

    with jax.named_scope("screen"):
        place = z * width + lax.axis_index(PLANE) * count
        unit = (lax.iota(jnp.int32, count)[:, None] + place) == lax.iota(jnp.int32, panel)[None, :]
        total = unit.astype(F32) + total
        high, rest = two_parts(total)
        screened = jnp.dot(
            jnp.concatenate([high, rest], axis=0), inv_high, preferred_element_type=F32
        )
        screened = screened[:count] + screened[count:]
        screened = screened + jnp.dot(high, inv_rest, preferred_element_type=F32)

    with jax.named_scope("gather_y"):
        low = screened.astype(LOW)
        gathered = jnp.concatenate([low] + [shift(low, Y, ny, k) for k in steps[1:]], axis=0)
        gathered = jnp.concatenate([gathered, swap(gathered)], axis=0)
        by_y = factors.reshape(ny, 2, count, -1)
        ordered = jnp.concatenate(
            [
                lax.dynamic_slice(by_y, ((y - k) % ny, c, 0, 0), (1, 1, count, nx * own))
                for c in (core, 1 - core)
                for k in steps
            ]
        ).reshape(-1, nx * own)

    with jax.named_scope("sigma"):
        products = lax.dot_general(
            gathered, panels, (((1,), (1,)), ((), ())), preferred_element_type=F32
        )
        local = -jnp.sum(products * ordered.astype(F32), axis=0).reshape(nx, own)
        back = (x - lax.iota(jnp.int32, nx)) % nx
        by_x = sum(
            jnp.where((back == k)[:, None], local[i][None], 0.0) for i, k in enumerate(steps)
        )
        copies = jnp.broadcast_to(by_x[:, None], (nx, nz, own)).reshape(-1, own)
        terms = lax.all_to_all(copies, (X, Z), 0, 0, tiled=True)
        sigma = jnp.sum(terms, axis=0)
    return sigma, screened[None]


def solution(mesh):
    split = Mesh(mesh.devices.reshape(2, 4, 2, 2, 8), ("grp", "x", "ylo", "core", "col"))
    return jax.shard_map(
        body,
        mesh=split,
        in_specs=(P(PLANE, Z), P(PLANE), P()),
        out_specs=(P(PLANE), P(Z, PLANE, None)),
        check_vma=False,
    )
```

```python
import jax
import jax.numpy as jnp
from jax import lax
from jax.sharding import Mesh, PartitionSpec as P

X, Y, Z, CORE = "x", ("grp", "ylo"), "col", "core"
PLANE = ("grp", "x", "ylo", "core")
LOW, F32 = jnp.bfloat16, jnp.float32
def shift(value, axis, size, step):
    return lax.ppermute(value, axis, [(i, (i + step) % size) for i in range(size)])


def along_z(value, *pairs):
    return lax.ppermute(value, Z, pairs)


def swap(value):
    return lax.ppermute(value, CORE, [(0, 1), (1, 0)])


def parts_of(value):
    out = []
    for _ in range(3):
        part = lax.reduce_precision(value, 8, 7)
        out.append(part.astype(LOW))
        value = value - part
    return out


def two_parts(value):
    high = lax.reduce_precision(value, 8, 7)
    return high.astype(LOW), (value - high).astype(LOW)


def body(orbital_b, gaps, block_inverse):
    own, width = orbital_b.shape
    panel = block_inverse.shape[0]
    nx, ny, nz = lax.axis_size(X), lax.axis_size(Y), lax.axis_size(Z)
    x, y, z, core = (lax.axis_index(a) for a in (X, Y, Z, CORE))
    count = width // lax.axis_size(PLANE)
    steps = (0, 2, 1, 3)

    with jax.named_scope("panel_z"):
        piece = orbital_b[:, :panel]
        one = along_z(piece, (0, 1))
        first, one = lax.optimization_barrier((piece, one))
        far_b = along_z(first, (0, 6))
        far_a = along_z(first, (0, 3))

    with jax.named_scope("blocks"):
        weight = 2.0 * gaps / (gaps * gaps + 1.0)
        extra = jnp.concatenate(
            [jnp.stack(parts_of(weight)), jnp.zeros((13, own), LOW)], axis=0
        )
        blocks = orbital_b.T.reshape(2, nx, -1, own)

        def rows_of(i):
            block = lax.dynamic_index_in_dim(blocks, i, 1, False).reshape(-1, own)
            return jnp.concatenate([block, extra], axis=0)

        rows = [rows_of((x + k) % nx) for k in steps]
        factors = [rows[0]] + [shift(row, X, nx, k) for row, k in zip(rows[1:], steps[1:])]

    with jax.named_scope("panel_z"):
        far_a, far_b, block_inverse, *_ = lax.optimization_barrier(
            (far_a, far_b, block_inverse, *rows)
        )
        two = along_z(one, (1, 2))
        first, far_b = lax.optimization_barrier((first, far_b))
        seven = along_z(first, (0, 7))
        held = jnp.where(z == 6, far_b, jnp.where(z == 3, far_a, piece))
        near = along_z(held, (3, 4), (6, 5))
        inv_high, inv_rest = two_parts(block_inverse)
        near, inv_high, inv_rest, *factors = lax.optimization_barrier(
            (near, inv_high, inv_rest, *factors)
        )
        held = jnp.where(z == 1, one, jnp.where(z == 2, two, jnp.where(z == 7, seven, held)))
        held = jnp.where((z == 4) | (z == 5), near, held)

    with jax.named_scope("panel_x"):
        panels = [held] + [shift(held, X, nx, k) for k in steps[1:]]
        panels = jnp.concatenate(panels, axis=0)

    with jax.named_scope("response"):
        factors = jnp.concatenate(factors, axis=1)
        weight = jnp.sum(factors[-16:-13].astype(F32), axis=0)
        factors = factors[:-16]
        weighted = (weight[:, None] * panels.astype(F32)).astype(LOW)
        part = jnp.dot(factors, weighted, preferred_element_type=F32)

    with jax.named_scope("sum_core"):
        part = part.reshape(ny, 2, count, panel)
        sent = lax.dynamic_index_in_dim(part, 1 - core, 1, False)
        kept = lax.dynamic_index_in_dim(part, core, 1, False) + swap(sent)

    with jax.named_scope("sum_y"):
        total = lax.dynamic_index_in_dim(kept, y, 0, False)
        for k in (2, 1, 3):
            piece = lax.dynamic_index_in_dim(kept, (y + k) % ny, 0, False).astype(LOW)
            total = total + shift(piece, Y, ny, k).astype(F32)

    with jax.named_scope("screen"):
        place = z * width + lax.axis_index(PLANE) * count
        unit = (lax.iota(jnp.int32, count)[:, None] + place) == lax.iota(jnp.int32, panel)[None, :]
        total = unit.astype(F32) + total
        high, rest = two_parts(total)
        screened = jnp.dot(
            jnp.concatenate([high, rest], axis=0), inv_high, preferred_element_type=F32
        )
        screened = screened[:count] + screened[count:]
        screened = screened + jnp.dot(high, inv_rest, preferred_element_type=F32)

    with jax.named_scope("gather_y"):
        low = screened.astype(LOW)
        gathered = jnp.concatenate([low] + [shift(low, Y, ny, k) for k in steps[1:]], axis=0)
        gathered = jnp.concatenate([gathered, swap(gathered)], axis=0)
        by_y = factors.reshape(ny, 2, count, -1)
        ordered = jnp.concatenate(
            [
                lax.dynamic_slice(by_y, ((y - k) % ny, c, 0, 0), (1, 1, count, nx * own))
                for c in (core, 1 - core)
                for k in steps
            ]
        ).reshape(-1, nx * own)

    with jax.named_scope("sigma"):
        products = lax.dot_general(
            gathered, panels, (((1,), (1,)), ((), ())), preferred_element_type=F32
        )
        local = -jnp.sum(products * ordered.astype(F32), axis=0).reshape(nx, own)
        back = (x - lax.iota(jnp.int32, nx)) % nx
        by_x = sum(
            jnp.where((back == k)[:, None], local[i][None], 0.0) for i, k in enumerate(steps)
        )
        copies = jnp.broadcast_to(by_x[:, None], (nx, nz, own)).reshape(-1, own)
        terms = lax.all_to_all(copies, (X, Z), 0, 0, tiled=True)
        sigma = jnp.sum(terms, axis=0)
    return sigma, screened[None]


def solution(mesh):
    split = Mesh(mesh.devices.reshape(2, 4, 2, 2, 8), ("grp", "x", "ylo", "core", "col"))
    return jax.shard_map(
        body,
        mesh=split,
        in_specs=(P(PLANE, Z), P(PLANE), P()),
        out_specs=(P(PLANE), P(Z, PLANE, None)),
        check_vma=False,
    )
```

```python
import jax
import jax.numpy as jnp
from jax import lax
from jax.sharding import Mesh, PartitionSpec as P

X, Y, Z, CORE = "x", ("grp", "ylo"), "col", "core"
PLANE = ("grp", "x", "ylo", "core")
LOW, F32 = jnp.bfloat16, jnp.float32
def shift(value, axis, size, step):
    return lax.ppermute(value, axis, [(i, (i + step) % size) for i in range(size)])


def along_z(value, *pairs):
    return lax.ppermute(value, Z, pairs)


def swap(value):
    return lax.ppermute(value, CORE, [(0, 1), (1, 0)])


def parts_of(value):
    out = []
    for _ in range(3):
        part = lax.reduce_precision(value, 8, 7)
        out.append(part.astype(LOW))
        value = value - part
    return out


def two_parts(value):
    high = lax.reduce_precision(value, 8, 7)
    return high.astype(LOW), (value - high).astype(LOW)


def body(orbital_b, gaps, block_inverse):
    own, width = orbital_b.shape
    panel = block_inverse.shape[0]
    nx, ny, nz = lax.axis_size(X), lax.axis_size(Y), lax.axis_size(Z)
    x, y, z, core = (lax.axis_index(a) for a in (X, Y, Z, CORE))
    count = width // lax.axis_size(PLANE)
    steps = (0, 2, 1, 3)

    with jax.named_scope("panel_z"):
        piece = orbital_b[:, :panel]
        far_a = along_z(piece, (0, 3))
        far_b = along_z(piece, (0, 6))

    with jax.named_scope("blocks"):
        weight = 2.0 * gaps / (gaps * gaps + 1.0)
        extra = jnp.concatenate(
            [jnp.stack(parts_of(weight)), jnp.zeros((13, own), LOW)], axis=0
        )
        blocks = orbital_b.T.reshape(2, nx, -1, own)

        def rows_of(i):
            block = lax.dynamic_index_in_dim(blocks, i, 1, False).reshape(-1, own)
            return jnp.concatenate([block, extra], axis=0)

        rows = [rows_of((x + k) % nx) for k in steps]
        factors = [rows[0]] + [shift(row, X, nx, k) for row, k in zip(rows[1:], steps[1:])]

    with jax.named_scope("panel_z"):
        far_a, far_b, block_inverse, *_ = lax.optimization_barrier(
            (far_a, far_b, block_inverse, *rows)
        )
        held = jnp.where(z == 3, far_a, jnp.where(z == 6, far_b, piece))
        near_a = along_z(held, (0, 7), (3, 4), (6, 5))
        near_b = along_z(held, (0, 1), (3, 2))
        inv_high, inv_rest = two_parts(block_inverse)
        near_a, near_b, inv_high, inv_rest, *factors = lax.optimization_barrier(
            (near_a, near_b, inv_high, inv_rest, *factors)
        )
        held = jnp.where((z == 7) | (z == 4) | (z == 5), near_a, held)
        held = jnp.where((z == 1) | (z == 2), near_b, held)

    with jax.named_scope("panel_x"):
        panels = [held] + [shift(held, X, nx, k) for k in steps[1:]]
        panels = jnp.concatenate(panels, axis=0)

    with jax.named_scope("response"):
        factors = jnp.concatenate(factors, axis=1)
        weight = jnp.sum(factors[-16:-13].astype(F32), axis=0)
        factors = factors[:-16]
        weighted = (weight[:, None] * panels.astype(F32)).astype(LOW)
        part = jnp.dot(factors, weighted, preferred_element_type=F32)

    with jax.named_scope("sum_core"):
        part = part.reshape(ny, 2, count, panel)
        sent = lax.dynamic_index_in_dim(part, 1 - core, 1, False).astype(LOW)
        kept = lax.dynamic_index_in_dim(part, core, 1, False) + swap(sent).astype(F32)

    with jax.named_scope("sum_y"):
        total = lax.dynamic_index_in_dim(kept, y, 0, False)
        for k in (2, 1, 3):
            piece = lax.dynamic_index_in_dim(kept, (y + k) % ny, 0, False).astype(LOW)
            total = total + shift(piece, Y, ny, k).astype(F32)

    with jax.named_scope("screen"):
        place = z * width + lax.axis_index(PLANE) * count
        unit = (lax.iota(jnp.int32, count)[:, None] + place) == lax.iota(jnp.int32, panel)[None, :]
        total = unit.astype(F32) + total
        high, rest = two_parts(total)
        screened = jnp.dot(
            jnp.concatenate([high, rest], axis=0), inv_high, preferred_element_type=F32
        )
        screened = screened[:count] + screened[count:]
        screened = screened + jnp.dot(high, inv_rest, preferred_element_type=F32)

    with jax.named_scope("gather_y"):
        low = screened.astype(LOW)
        gathered = jnp.concatenate([low] + [shift(low, Y, ny, k) for k in steps[1:]], axis=0)
        gathered = jnp.concatenate([gathered, swap(gathered)], axis=0)
        by_y = factors.reshape(ny, 2, count, -1)
        ordered = jnp.concatenate(
            [
                lax.dynamic_slice(by_y, ((y - k) % ny, c, 0, 0), (1, 1, count, nx * own))
                for c in (core, 1 - core)
                for k in steps
            ]
        ).reshape(-1, nx * own)

    with jax.named_scope("sigma"):
        products = lax.dot_general(
            gathered, panels, (((1,), (1,)), ((), ())), preferred_element_type=F32
        )
        local = -jnp.sum(products * ordered.astype(F32), axis=0).reshape(nx, own)
        back = (x - lax.iota(jnp.int32, nx)) % nx
        by_x = sum(
            jnp.where((back == k)[:, None], local[i][None], 0.0) for i, k in enumerate(steps)
        )
        copies = jnp.broadcast_to(by_x[:, None], (nx, nz, own)).reshape(-1, own)
        terms = lax.all_to_all(copies, (X, Z), 0, 0, tiled=True)
        sigma = jnp.sum(terms, axis=0)
    return sigma, screened[None]


def solution(mesh):
    split = Mesh(mesh.devices.reshape(2, 4, 2, 2, 8), ("grp", "x", "ylo", "core", "col"))
    return jax.shard_map(
        body,
        mesh=split,
        in_specs=(P(PLANE, Z), P(PLANE), P()),
        out_specs=(P(PLANE), P(Z, PLANE, None)),
        check_vma=False,
    )
```

```python
import jax
import jax.numpy as jnp
from jax import lax
from jax.sharding import Mesh, PartitionSpec as P

X, Y, Z, CORE = "x", ("grp", "ylo"), "col", "core"
PLANE = ("grp", "x", "ylo", "core")
LOW, F32 = jnp.bfloat16, jnp.float32
def shift(value, axis, size, step):
    return lax.ppermute(value, axis, [(i, (i + step) % size) for i in range(size)])


def along_z(value, *pairs):
    return lax.ppermute(value, Z, pairs)


def swap(value):
    return lax.ppermute(value, CORE, [(0, 1), (1, 0)])


def parts_of(value):
    out = []
    for _ in range(3):
        part = lax.reduce_precision(value, 8, 7)
        out.append(part.astype(LOW))
        value = value - part
    return out


def two_parts(value):
    high = lax.reduce_precision(value, 8, 7)
    return high.astype(LOW), (value - high).astype(LOW)


def body(orbital_b, gaps, block_inverse):
    own, width = orbital_b.shape
    panel = block_inverse.shape[0]
    nx, ny, nz = lax.axis_size(X), lax.axis_size(Y), lax.axis_size(Z)
    x, y, z, core = (lax.axis_index(a) for a in (X, Y, Z, CORE))
    count = width // lax.axis_size(PLANE)
    steps = (0, 2, 1, 3)

    with jax.named_scope("panel_z"):
        piece = orbital_b[:, :panel]
        far_a = along_z(piece, (0, 3))
        far_b = along_z(piece, (0, 6))

    with jax.named_scope("blocks"):
        weight = 2.0 * gaps / (gaps * gaps + 1.0)
        extra = jnp.concatenate(
            [jnp.stack(parts_of(weight)), jnp.zeros((13, own), LOW)], axis=0
        )
        blocks = orbital_b.T.reshape(2, nx, -1, own)

        def rows_of(i):
            block = lax.dynamic_index_in_dim(blocks, i, 1, False).reshape(-1, own)
            return jnp.concatenate([block, extra], axis=0)

        rows = [rows_of((x + k) % nx) for k in steps]
        factors = [rows[0]] + [shift(row, X, nx, k) for row, k in zip(rows[1:], steps[1:])]

    with jax.named_scope("panel_z"):
        far_a, far_b, block_inverse, *_ = lax.optimization_barrier(
            (far_a, far_b, block_inverse, *rows)
        )
        held = jnp.where(z == 3, far_a, jnp.where(z == 6, far_b, piece))
        near_a = along_z(held, (0, 7), (3, 4), (6, 5))
        near_b = along_z(held, (0, 1), (3, 2))
        inv_high, inv_rest = two_parts(block_inverse)
        near_a, near_b, inv_high, inv_rest, *factors = lax.optimization_barrier(
            (near_a, near_b, inv_high, inv_rest, *factors)
        )
        held = jnp.where((z == 7) | (z == 4) | (z == 5), near_a, held)
        held = jnp.where((z == 1) | (z == 2), near_b, held)

    with jax.named_scope("panel_x"):
        panels = [held] + [shift(held, X, nx, k) for k in steps[1:]]
        panels = jnp.concatenate(panels, axis=0)

    with jax.named_scope("response"):
        factors = jnp.concatenate(factors, axis=1)
        weight = jnp.sum(factors[-16:-13].astype(F32), axis=0)
        factors = factors[:-16]
        weighted = (weight[:, None] * panels.astype(F32)).astype(LOW)
        part = jnp.dot(factors, weighted, preferred_element_type=F32)

    with jax.named_scope("sum_core"):
        part = part.reshape(ny, 2, count, panel)
        sent = lax.dynamic_index_in_dim(part, 1 - core, 1, False).astype(LOW)
        kept = lax.dynamic_index_in_dim(part, core, 1, False) + swap(sent).astype(F32)

    with jax.named_scope("sum_y"):
        total = lax.dynamic_index_in_dim(kept, y, 0, False)
        for k in (2, 1, 3):
            piece = lax.dynamic_index_in_dim(kept, (y + k) % ny, 0, False).astype(LOW)
            total = total + shift(piece, Y, ny, k).astype(F32)

    with jax.named_scope("inverse_factors"):
        inverse_factors = sum(
            lax.dot_general(panels, part, (((1,), (1,)), ((), ())), preferred_element_type=F32)
            for part in (inv_high, inv_rest)
        ).astype(LOW)

    with jax.named_scope("screen"):
        place = z * width + lax.axis_index(PLANE) * count
        unit = (lax.iota(jnp.int32, count)[:, None] + place) == lax.iota(jnp.int32, panel)[None, :]
        total = unit.astype(F32) + total
        high, rest = two_parts(total)
        screened = jnp.dot(
            jnp.concatenate([high, rest], axis=0), inv_high, preferred_element_type=F32
        )
        screened = screened[:count] + screened[count:]
        screened = screened + jnp.dot(high, inv_rest, preferred_element_type=F32)

    with jax.named_scope("gather_y"):
        gathered = jnp.concatenate([high] + [shift(high, Y, ny, k) for k in steps[1:]], axis=0)
        gathered, inverse_factors = lax.optimization_barrier((gathered, inverse_factors))
        gathered = jnp.concatenate([gathered, swap(gathered)], axis=0)
        by_y = factors.reshape(ny, 2, count, -1)
        ordered = jnp.concatenate(
            [
                lax.dynamic_slice(by_y, ((y - k) % ny, c, 0, 0), (1, 1, count, nx * own))
                for c in (core, 1 - core)
                for k in steps
            ]
        ).reshape(-1, nx * own)

    with jax.named_scope("sigma"):
        products = lax.dot_general(
            gathered, inverse_factors, (((1,), (1,)), ((), ())), preferred_element_type=F32
        )
        local = -jnp.sum(products * ordered.astype(F32), axis=0).reshape(nx, own)
        back = (x - lax.iota(jnp.int32, nx)) % nx
        by_x = sum(
            jnp.where((back == k)[:, None], local[i][None], 0.0) for i, k in enumerate(steps)
        )
        copies = jnp.broadcast_to(by_x[:, None], (nx, nz, own)).reshape(-1, own)
        terms = lax.all_to_all(copies, (X, Z), 0, 0, tiled=True)
        sigma = jnp.sum(terms, axis=0)
    return sigma, screened[None]


def solution(mesh):
    split = Mesh(mesh.devices.reshape(2, 4, 2, 2, 8), ("grp", "x", "ylo", "core", "col"))
    return jax.shard_map(
        body,
        mesh=split,
        in_specs=(P(PLANE, Z), P(PLANE), P()),
        out_specs=(P(PLANE), P(Z, PLANE, None)),
        check_vma=False,
    )
```

```python
import jax
import jax.numpy as jnp
from jax import lax
from jax.sharding import Mesh, PartitionSpec as P

X, Y, Z, CORE = "x", ("grp", "ylo"), "col", "core"
PLANE = ("grp", "x", "ylo", "core")
LOW, F32 = jnp.bfloat16, jnp.float32
def shift(value, axis, size, step):
    return lax.ppermute(value, axis, [(i, (i + step) % size) for i in range(size)])


def along_z(value, *pairs):
    return lax.ppermute(value, Z, pairs)


def swap(value):
    return lax.ppermute(value, CORE, [(0, 1), (1, 0)])


def parts_of(value):
    out = []
    for _ in range(3):
        part = lax.reduce_precision(value, 8, 7)
        out.append(part.astype(LOW))
        value = value - part
    return out


def two_parts(value):
    high = lax.reduce_precision(value, 8, 7)
    return high.astype(LOW), (value - high).astype(LOW)


def body(orbital_b, gaps, block_inverse):
    own, width = orbital_b.shape
    panel = block_inverse.shape[0]
    nx, ny, nz = lax.axis_size(X), lax.axis_size(Y), lax.axis_size(Z)
    x, y, z, core = (lax.axis_index(a) for a in (X, Y, Z, CORE))
    count = width // lax.axis_size(PLANE)
    steps = (0, 2, 1, 3)

    with jax.named_scope("panel_z"):
        piece = orbital_b[:, :panel]
        far_a = along_z(piece, (0, 3))
        far_b = along_z(piece, (0, 6))

    with jax.named_scope("blocks"):
        weight = 2.0 * gaps / (gaps * gaps + 1.0)
        extra = jnp.concatenate(
            [jnp.stack(parts_of(weight)), jnp.zeros((13, own), LOW)], axis=0
        )
        blocks = orbital_b.T.reshape(2, nx, -1, own)

        def rows_of(i):
            block = lax.dynamic_index_in_dim(blocks, i, 1, False).reshape(-1, own)
            return jnp.concatenate([block, extra], axis=0)

        rows = [rows_of((x + k) % nx) for k in steps]
        factors = [rows[0]] + [shift(row, X, nx, k) for row, k in zip(rows[1:], steps[1:])]

    with jax.named_scope("panel_z"):
        far_a, far_b, block_inverse, *_ = lax.optimization_barrier(
            (far_a, far_b, block_inverse, *rows)
        )
        held = jnp.where(z == 3, far_a, jnp.where(z == 6, far_b, piece))
        near_a = along_z(held, (0, 7), (3, 4), (6, 5))
        near_b = along_z(held, (0, 1), (3, 2))
        inv_high, inv_rest = two_parts(block_inverse)
        near_a, near_b, inv_high, inv_rest, *factors = lax.optimization_barrier(
            (near_a, near_b, inv_high, inv_rest, *factors)
        )
        held = jnp.where((z == 7) | (z == 4) | (z == 5), near_a, held)
        held = jnp.where((z == 1) | (z == 2), near_b, held)

    with jax.named_scope("panel_x"):
        panels = [held] + [shift(held, X, nx, k) for k in steps[1:]]
        panels = jnp.concatenate(panels, axis=0)

    with jax.named_scope("response"):
        factors = jnp.concatenate(factors, axis=1)
        weight = jnp.sum(factors[-16:-13].astype(F32), axis=0)
        factors = factors[:-16]
        weighted = (weight[:, None] * panels.astype(F32)).astype(LOW)
        part = jnp.dot(factors, weighted, preferred_element_type=F32)

    with jax.named_scope("sum_core"):
        part = part.reshape(ny, 2, count, panel)
        sent = lax.dynamic_index_in_dim(part, 1 - core, 1, False).astype(LOW)
        kept = lax.dynamic_index_in_dim(part, core, 1, False) + swap(sent).astype(F32)

    with jax.named_scope("sum_y"):
        total = lax.dynamic_index_in_dim(kept, y, 0, False)
        for k in (2, 1, 3):
            piece = lax.dynamic_index_in_dim(kept, (y + k) % ny, 0, False).astype(LOW)
            total = total + shift(piece, Y, ny, k).astype(F32)

    with jax.named_scope("inverse_factors"):
        inverse_factors = two_parts(
            sum(
                lax.dot_general(panels, part, (((1,), (1,)), ((), ())), preferred_element_type=F32)
                for part in (inv_high, inv_rest)
            )
        )

    with jax.named_scope("screen"):
        place = z * width + lax.axis_index(PLANE) * count
        unit = (lax.iota(jnp.int32, count)[:, None] + place) == lax.iota(jnp.int32, panel)[None, :]
        total = unit.astype(F32) + total
        high, rest = two_parts(total)
        screened = jnp.dot(
            jnp.concatenate([high, rest], axis=0), inv_high, preferred_element_type=F32
        )
        screened = screened[:count] + screened[count:]
        screened = screened + jnp.dot(high, inv_rest, preferred_element_type=F32)

    with jax.named_scope("gather_y"):
        gathered = jnp.concatenate([high] + [shift(high, Y, ny, k) for k in steps[1:]], axis=0)
        gathered, inverse_factors, screened = lax.optimization_barrier(
            (gathered, inverse_factors, screened)
        )
        gathered = jnp.concatenate([gathered, swap(gathered)], axis=0)
        by_y = factors.reshape(ny, 2, count, -1)
        ordered = jnp.concatenate(
            [
                lax.dynamic_slice(by_y, ((y - k) % ny, c, 0, 0), (1, 1, count, nx * own))
                for c in (core, 1 - core)
                for k in steps
            ]
        ).reshape(-1, nx * own)

    with jax.named_scope("sigma"):
        products = sum(
            lax.dot_general(gathered, part, (((1,), (1,)), ((), ())), preferred_element_type=F32)
            for part in inverse_factors
        )
        local = -jnp.sum(products * ordered.astype(F32), axis=0).reshape(nx, own)
        back = (x - lax.iota(jnp.int32, nx)) % nx
        by_x = sum(
            jnp.where((back == k)[:, None], local[i][None], 0.0) for i, k in enumerate(steps)
        )
        copies = jnp.broadcast_to(by_x[:, None], (nx, nz, own)).reshape(-1, own)
        terms = lax.all_to_all(copies, (X, Z), 0, 0, tiled=True)
        sigma = jnp.sum(terms, axis=0)
    return sigma, screened[None]


def solution(mesh):
    split = Mesh(mesh.devices.reshape(2, 4, 2, 2, 8), ("grp", "x", "ylo", "core", "col"))
    return jax.shard_map(
        body,
        mesh=split,
        in_specs=(P(PLANE, Z), P(PLANE), P()),
        out_specs=(P(PLANE), P(Z, PLANE, None)),
        check_vma=False,
    )
```

```python
import jax
import jax.numpy as jnp
from jax import lax
from jax.sharding import Mesh, PartitionSpec as P

X, Y, Z, CORE = "x", ("grp", "ylo"), "col", "core"
PLANE = ("grp", "x", "ylo", "core")
LOW, F32 = jnp.bfloat16, jnp.float32
def shift(value, axis, size, step):
    return lax.ppermute(value, axis, [(i, (i + step) % size) for i in range(size)])


def along_z(value, *pairs):
    return lax.ppermute(value, Z, pairs)


def swap(value):
    return lax.ppermute(value, CORE, [(0, 1), (1, 0)])


def parts_of(value):
    out = []
    for _ in range(3):
        part = lax.reduce_precision(value, 8, 7)
        out.append(part.astype(LOW))
        value = value - part
    return out


def two_parts(value):
    high = lax.reduce_precision(value, 8, 7)
    return high.astype(LOW), (value - high).astype(LOW)


def body(orbital_b, gaps, block_inverse):
    own, width = orbital_b.shape
    panel = block_inverse.shape[0]
    nx, ny, nz = lax.axis_size(X), lax.axis_size(Y), lax.axis_size(Z)
    x, y, z, core = (lax.axis_index(a) for a in (X, Y, Z, CORE))
    count = width // lax.axis_size(PLANE)
    steps = (0, 2, 1, 3)

    with jax.named_scope("panel_z"):
        piece = orbital_b[:, :panel]
        far_a = along_z(piece, (0, 3))
        far_b = along_z(piece, (0, 6))

    with jax.named_scope("blocks"):
        weight = 2.0 * gaps / (gaps * gaps + 1.0)
        extra = jnp.concatenate(
            [jnp.stack(parts_of(weight)), jnp.zeros((13, own), LOW)], axis=0
        )
        blocks = orbital_b.T.reshape(2, nx, -1, own)

        def rows_of(i):
            block = lax.dynamic_index_in_dim(blocks, i, 1, False).reshape(-1, own)
            return jnp.concatenate([block, extra], axis=0)

        rows = [rows_of((x + k) % nx) for k in steps]
        factors = [rows[0]] + [shift(row, X, nx, k) for row, k in zip(rows[1:], steps[1:])]

    with jax.named_scope("panel_z"):
        far_a, far_b, block_inverse, *_ = lax.optimization_barrier(
            (far_a, far_b, block_inverse, *rows)
        )
        held = jnp.where(z == 3, far_a, jnp.where(z == 6, far_b, piece))
        near_a = along_z(held, (0, 7), (3, 4), (6, 5))
        near_b = along_z(held, (0, 1), (3, 2))
        inv_high, inv_rest = two_parts(block_inverse)
        near_a, near_b, inv_high, inv_rest, *factors = lax.optimization_barrier(
            (near_a, near_b, inv_high, inv_rest, *factors)
        )
        held = jnp.where((z == 7) | (z == 4) | (z == 5), near_a, held)
        held = jnp.where((z == 1) | (z == 2), near_b, held)

    with jax.named_scope("panel_x"):
        blocks = [held] + [shift(held, X, nx, k) for k in steps[1:]]
        panels = jnp.concatenate(blocks, axis=0)

    with jax.named_scope("response"):
        factors = jnp.concatenate(factors, axis=1)
        weight = jnp.sum(factors[-16:-13].astype(F32), axis=0)
        factors = factors[:-16]
        weighted = (weight[:, None] * panels.astype(F32)).astype(LOW)
        by_core = factors.reshape(ny, 2, count, -1)
        theirs, mine = (
            lax.dynamic_index_in_dim(by_core, c, 1, False).reshape(ny * count, -1)
            for c in (1 - core, core)
        )
        sent = jnp.dot(theirs, weighted, preferred_element_type=F32).astype(LOW)
        kept = jnp.dot(mine, weighted, preferred_element_type=F32)
        kept, sent = lax.optimization_barrier((kept, swap(sent)))
        kept = (kept + sent.astype(F32)).reshape(ny, count, panel)
        kept, *blocks = lax.optimization_barrier((kept, *blocks))

    with jax.named_scope("sum_y"):
        total = lax.dynamic_index_in_dim(kept, y, 0, False)
        for k in (2, 1, 3):
            piece = lax.dynamic_index_in_dim(kept, (y + k) % ny, 0, False).astype(LOW)
            total = total + shift(piece, Y, ny, k).astype(F32)

    with jax.named_scope("inverse_factors"):
        panels = jnp.concatenate(blocks, axis=0)
        inverse_factors = sum(
            lax.dot_general(panels, part, (((1,), (1,)), ((), ())), preferred_element_type=F32)
            for part in (inv_high, inv_rest)
        )
        inverse_factors = jnp.concatenate(two_parts(inverse_factors), axis=0)

    with jax.named_scope("screen"):
        place = z * width + lax.axis_index(PLANE) * count
        unit = (lax.iota(jnp.int32, count)[:, None] + place) == lax.iota(jnp.int32, panel)[None, :]
        total = unit.astype(F32) + total
        high, rest = two_parts(total)
        screened = jnp.dot(
            jnp.concatenate([high, rest], axis=0), inv_high, preferred_element_type=F32
        )
        screened = screened[:count] + screened[count:]
        screened = screened + jnp.dot(high, inv_rest, preferred_element_type=F32)

    with jax.named_scope("gather_y"):
        gathered = jnp.concatenate([high] + [shift(high, Y, ny, k) for k in steps[1:]], axis=0)
        gathered, inverse_factors, screened = lax.optimization_barrier(
            (gathered, inverse_factors, screened)
        )
        gathered = jnp.concatenate([gathered, swap(gathered)], axis=0)
        by_y = factors.reshape(ny, 2, count, -1)
        ordered = jnp.concatenate(
            [
                lax.dynamic_slice(by_y, ((y - k) % ny, c, 0, 0), (1, 1, count, nx * own))
                for c in (core, 1 - core)
                for k in steps
            ]
        ).reshape(-1, nx * own)

    with jax.named_scope("sigma"):
        products = lax.dot_general(
            gathered, inverse_factors, (((1,), (1,)), ((), ())), preferred_element_type=F32
        )
        ordered = jnp.concatenate([ordered, ordered], axis=1).astype(F32)
        local = -jnp.sum(products * ordered, axis=0).reshape(2, nx, own)
        local = local[0] + local[1]
        back = (x - lax.iota(jnp.int32, nx)) % nx
        by_x = sum(
            jnp.where((back == k)[:, None], local[i][None], 0.0) for i, k in enumerate(steps)
        )
        copies = jnp.broadcast_to(by_x[:, None], (nx, nz, own)).reshape(-1, own)
        terms = lax.all_to_all(copies, (X, Z), 0, 0, tiled=True)
        sigma = jnp.sum(terms, axis=0)
    return sigma, screened[None]


def solution(mesh):
    split = Mesh(mesh.devices.reshape(2, 4, 2, 2, 8), ("grp", "x", "ylo", "core", "col"))
    return jax.shard_map(
        body,
        mesh=split,
        in_specs=(P(PLANE, Z), P(PLANE), P()),
        out_specs=(P(PLANE), P(Z, PLANE, None)),
        check_vma=False,
    )
```

```python
import jax
import jax.numpy as jnp
from jax import lax
from jax.sharding import Mesh, PartitionSpec as P

X, Y, Z, CORE = "x", ("grp", "ylo"), "col", "core"
PLANE = ("grp", "x", "ylo", "core")
LOW, F32 = jnp.bfloat16, jnp.float32
def shift(value, axis, size, step):
    return lax.ppermute(value, axis, [(i, (i + step) % size) for i in range(size)])


def along_z(value, *pairs):
    return lax.ppermute(value, Z, pairs)


def swap(value):
    return lax.ppermute(value, CORE, [(0, 1), (1, 0)])


def parts_of(value):
    out = []
    for _ in range(3):
        part = lax.reduce_precision(value, 8, 7)
        out.append(part.astype(LOW))
        value = value - part
    return out


def two_parts(value):
    high = lax.reduce_precision(value, 8, 7)
    return high.astype(LOW), (value - high).astype(LOW)


def body(orbital_b, gaps, block_inverse):
    own, width = orbital_b.shape
    panel = block_inverse.shape[0]
    nx, ny, nz = lax.axis_size(X), lax.axis_size(Y), lax.axis_size(Z)
    x, y, z, core = (lax.axis_index(a) for a in (X, Y, Z, CORE))
    count = width // lax.axis_size(PLANE)
    steps = (0, 2, 1, 3)

    with jax.named_scope("panel_z"):
        piece = orbital_b[:, :panel]
        far_a = along_z(piece, (0, 3))
        far_b = along_z(piece, (0, 6))

    with jax.named_scope("blocks"):
        weight = 2.0 * gaps / (gaps * gaps + 1.0)
        extra = jnp.concatenate(
            [jnp.stack(parts_of(weight)), jnp.zeros((13, own), LOW)], axis=0
        )
        blocks = orbital_b.T.reshape(2, nx, -1, own)

        def rows_of(i):
            block = lax.dynamic_index_in_dim(blocks, i, 1, False).reshape(-1, own)
            return jnp.concatenate([block, extra], axis=0)

        rows = [rows_of((x + k) % nx) for k in steps]
        factors = [rows[0]] + [shift(row, X, nx, k) for row, k in zip(rows[1:], steps[1:])]

    with jax.named_scope("panel_z"):
        far_a, far_b, block_inverse, *_ = lax.optimization_barrier(
            (far_a, far_b, block_inverse, *rows)
        )
        held = jnp.where(z == 3, far_a, jnp.where(z == 6, far_b, piece))
        near_a = along_z(held, (0, 7), (3, 4), (6, 5))
        near_b = along_z(held, (0, 1), (3, 2))
        inv_high, inv_rest = two_parts(block_inverse)
        near_a, near_b, inv_high, inv_rest, *factors = lax.optimization_barrier(
            (near_a, near_b, inv_high, inv_rest, *factors)
        )
        held = jnp.where((z == 7) | (z == 4) | (z == 5), near_a, held)
        held = jnp.where((z == 1) | (z == 2), near_b, held)

    with jax.named_scope("panel_x"):
        blocks = [held] + [shift(held, X, nx, k) for k in steps[1:]]
        panels = jnp.concatenate(blocks, axis=0)

    with jax.named_scope("response"):
        factors = jnp.concatenate(factors, axis=1)
        weight = jnp.sum(factors[-16:-13].astype(F32), axis=0)
        factors = factors[:-16]
        weighted = (weight[:, None] * panels.astype(F32)).astype(LOW)
        by_core = factors.reshape(ny, 2, count, -1)
        theirs, mine = (
            lax.dynamic_index_in_dim(by_core, c, 1, False).reshape(ny * count, -1)
            for c in (1 - core, core)
        )
        sent = jnp.dot(theirs, weighted, preferred_element_type=F32).astype(LOW)
        kept = jnp.dot(mine, weighted, preferred_element_type=F32)
        kept, sent = lax.optimization_barrier((kept, swap(sent)))
        kept = (kept + sent.astype(F32)).reshape(ny, count, panel)
        kept, *blocks = lax.optimization_barrier((kept, *blocks))

    with jax.named_scope("sum_y"):
        total = lax.dynamic_index_in_dim(kept, y, 0, False)
        for k in (2, 1, 3):
            piece = lax.dynamic_index_in_dim(kept, (y + k) % ny, 0, False).astype(LOW)
            total = total + shift(piece, Y, ny, k).astype(F32)

    with jax.named_scope("inverse_factors"):
        panels = jnp.concatenate(blocks, axis=0)
        inverse_factors = sum(
            lax.dot_general(panels, part, (((1,), (1,)), ((), ())), preferred_element_type=F32)
            for part in (inv_high, inv_rest)
        )
        inverse_factors = jnp.concatenate(two_parts(inverse_factors), axis=0)

    with jax.named_scope("screen"):
        place = z * width + lax.axis_index(PLANE) * count
        unit = (lax.iota(jnp.int32, count)[:, None] + place) == lax.iota(jnp.int32, panel)[None, :]
        total = unit.astype(F32) + total
        high, rest = two_parts(total)
        screened = jnp.dot(
            jnp.concatenate([high, rest], axis=0), inv_high, preferred_element_type=F32
        )
        screened = screened[:count] + screened[count:]
        screened = screened + jnp.dot(high, inv_rest, preferred_element_type=F32)

    with jax.named_scope("gather_y"):
        gathered = jnp.concatenate([high] + [shift(high, Y, ny, k) for k in steps[1:]], axis=0)
        gathered, inverse_factors, screened = lax.optimization_barrier(
            (gathered, inverse_factors, screened)
        )
        by_y = factors.reshape(ny, 2, count, -1)
        ordered = [
            jnp.concatenate(
                [
                    lax.dynamic_slice(by_y, ((y - k) % ny, c, 0, 0), (1, 1, count, nx * own))
                    for k in steps
                ]
            ).reshape(-1, nx * own)
            for c in (core, 1 - core)
        ]

    with jax.named_scope("sigma"):

        def terms_of(rows, weights):
            products = lax.dot_general(
                rows, inverse_factors, (((1,), (1,)), ((), ())), preferred_element_type=F32
            )
            weights = jnp.concatenate([weights, weights], axis=1).astype(F32)
            return jnp.sum(products * weights, axis=0)

        local, other = lax.optimization_barrier((terms_of(gathered, ordered[0]), swap(gathered)))
        local = -(local + terms_of(other, ordered[1])).reshape(2, nx, own)
        local = local[0] + local[1]
        back = (x - lax.iota(jnp.int32, nx)) % nx
        by_x = sum(
            jnp.where((back == k)[:, None], local[i][None], 0.0) for i, k in enumerate(steps)
        )
        copies = jnp.broadcast_to(by_x[:, None], (nx, nz, own)).reshape(-1, own)
        terms = lax.all_to_all(copies, (X, Z), 0, 0, tiled=True)
        sigma = jnp.sum(terms, axis=0)
    return sigma, screened[None]


def solution(mesh):
    split = Mesh(mesh.devices.reshape(2, 4, 2, 2, 8), ("grp", "x", "ylo", "core", "col"))
    return jax.shard_map(
        body,
        mesh=split,
        in_specs=(P(PLANE, Z), P(PLANE), P()),
        out_specs=(P(PLANE), P(Z, PLANE, None)),
        check_vma=False,
    )
```

```python
import jax
import jax.numpy as jnp
from jax import lax
from jax.sharding import Mesh, PartitionSpec as P

X, Y, Z, CORE = "x", ("grp", "ylo"), "col", "core"
PLANE = ("grp", "x", "ylo", "core")
LOW, F32 = jnp.bfloat16, jnp.float32
def shift(value, axis, size, step):
    return lax.ppermute(value, axis, [(i, (i + step) % size) for i in range(size)])


def along_z(value, *pairs):
    return lax.ppermute(value, Z, pairs)


def turn(value, size, step):
    pairs = []
    for x in range(size):
        pairs += [(x * 2, (x + step) % size * 2), (x * 2 + 1, (x - step) % size * 2 + 1)]
    return lax.ppermute(value, (X, CORE), pairs)


def swap(value):
    return lax.ppermute(value, CORE, [(0, 1), (1, 0)])


def parts_of(value):
    out = []
    for _ in range(3):
        part = lax.reduce_precision(value, 8, 7)
        out.append(part.astype(LOW))
        value = value - part
    return out


def two_parts(value):
    high = lax.reduce_precision(value, 8, 7)
    return high.astype(LOW), (value - high).astype(LOW)


def body(orbital_b, gaps, block_inverse):
    own, width = orbital_b.shape
    panel = block_inverse.shape[0]
    nx, ny, nz = lax.axis_size(X), lax.axis_size(Y), lax.axis_size(Z)
    x, y, z, core = (lax.axis_index(a) for a in (X, Y, Z, CORE))
    count = width // lax.axis_size(PLANE)
    steps = (0, 2, 1, 3)
    way = 1 - 2 * core

    with jax.named_scope("panel_z"):
        piece = orbital_b[:, :panel]
        far_a = along_z(piece, (0, 3))
        far_b = along_z(piece, (0, 6))

    with jax.named_scope("blocks"):
        weight = 2.0 * gaps / (gaps * gaps + 1.0)
        extra = jnp.concatenate(
            [jnp.stack(parts_of(weight)), jnp.zeros((13, own), LOW)], axis=0
        )
        blocks = orbital_b.T.reshape(2, nx, -1, own)

        def rows_of(i):
            block = lax.dynamic_index_in_dim(blocks, i, 1, False).reshape(-1, own)
            return jnp.concatenate([block, extra], axis=0)

        rows = [rows_of((x + way * k) % nx) for k in steps]
        factors = [rows[0]] + [turn(row, nx, k) for row, k in zip(rows[1:], steps[1:])]

    with jax.named_scope("panel_z"):
        far_a, far_b, block_inverse, *_ = lax.optimization_barrier(
            (far_a, far_b, block_inverse, *rows)
        )
        held = jnp.where(z == 3, far_a, jnp.where(z == 6, far_b, piece))
        near_a = along_z(held, (0, 7), (3, 4), (6, 5))
        near_b = along_z(held, (0, 1), (3, 2))
        inv_high, inv_rest = two_parts(block_inverse)
        near_a, near_b, inv_high, inv_rest, *factors = lax.optimization_barrier(
            (near_a, near_b, inv_high, inv_rest, *factors)
        )
        held = jnp.where((z == 7) | (z == 4) | (z == 5), near_a, held)
        held = jnp.where((z == 1) | (z == 2), near_b, held)

    with jax.named_scope("panel_x"):
        blocks = [held] + [turn(held, nx, k) for k in steps[1:]]
        panels = jnp.concatenate(blocks, axis=0)

    with jax.named_scope("response"):
        factors = jnp.concatenate(factors, axis=1)
        weight = jnp.sum(factors[-16:-13].astype(F32), axis=0)
        factors = factors[:-16]
        weighted = (weight[:, None] * panels.astype(F32)).astype(LOW)
        by_core = factors.reshape(ny, 2, count, -1)
        theirs, mine = (
            lax.dynamic_index_in_dim(by_core, c, 1, False).reshape(ny * count, -1)
            for c in (1 - core, core)
        )
        sent = jnp.dot(theirs, weighted, preferred_element_type=F32).astype(LOW)
        kept = jnp.dot(mine, weighted, preferred_element_type=F32)
        kept, sent = lax.optimization_barrier((kept, swap(sent)))
        kept = (kept + sent.astype(F32)).reshape(ny, count, panel)
        kept, *blocks = lax.optimization_barrier((kept, *blocks))

    with jax.named_scope("sum_y"):
        total = lax.dynamic_index_in_dim(kept, y, 0, False)
        for k in (2, 1, 3):
            piece = lax.dynamic_index_in_dim(kept, (y + k) % ny, 0, False).astype(LOW)
            total = total + shift(piece, Y, ny, k).astype(F32)

    with jax.named_scope("inverse_factors"):
        panels = jnp.concatenate(blocks, axis=0)
        inverse_factors = sum(
            lax.dot_general(panels, part, (((1,), (1,)), ((), ())), preferred_element_type=F32)
            for part in (inv_high, inv_rest)
        )
        inverse_factors = jnp.concatenate(two_parts(inverse_factors), axis=0)

    with jax.named_scope("screen"):
        place = z * width + lax.axis_index(PLANE) * count
        unit = (lax.iota(jnp.int32, count)[:, None] + place) == lax.iota(jnp.int32, panel)[None, :]
        total = unit.astype(F32) + total
        high, rest = two_parts(total)
        screened = jnp.dot(
            jnp.concatenate([high, rest], axis=0), inv_high, preferred_element_type=F32
        )
        screened = screened[:count] + screened[count:]
        screened = screened + jnp.dot(high, inv_rest, preferred_element_type=F32)

    with jax.named_scope("gather_y"):
        gathered = jnp.concatenate([high] + [shift(high, Y, ny, k) for k in steps[1:]], axis=0)
        gathered, inverse_factors, screened = lax.optimization_barrier(
            (gathered, inverse_factors, screened)
        )
        gathered = jnp.concatenate([gathered, swap(gathered)], axis=0)
        by_y = factors.reshape(ny, 2, count, -1)
        ordered = jnp.concatenate(
            [
                lax.dynamic_slice(by_y, ((y - k) % ny, c, 0, 0), (1, 1, count, nx * own))
                for c in (core, 1 - core)
                for k in steps
            ]
        ).reshape(-1, nx * own)

    with jax.named_scope("sigma"):
        products = lax.dot_general(
            gathered, inverse_factors, (((1,), (1,)), ((), ())), preferred_element_type=F32
        )
        ordered = jnp.concatenate([ordered, ordered], axis=1).astype(F32)
        local = -jnp.sum(products * ordered, axis=0).reshape(2, nx, own)
        local = local[0] + local[1]
        back = way * (x - lax.iota(jnp.int32, nx)) % nx
        by_x = sum(
            jnp.where((back == k)[:, None], local[i][None], 0.0) for i, k in enumerate(steps)
        )
        copies = jnp.broadcast_to(by_x[:, None], (nx, nz, own)).reshape(-1, own)
        terms = lax.all_to_all(copies, (X, Z), 0, 0, tiled=True)
        sigma = jnp.sum(terms, axis=0)
    return sigma, screened[None]


def solution(mesh):
    split = Mesh(mesh.devices.reshape(2, 4, 2, 2, 8), ("grp", "x", "ylo", "core", "col"))
    return jax.shard_map(
        body,
        mesh=split,
        in_specs=(P(PLANE, Z), P(PLANE), P()),
        out_specs=(P(PLANE), P(Z, PLANE, None)),
        check_vma=False,
    )
```

```python
import jax
import jax.numpy as jnp
from jax import lax
from jax.sharding import Mesh, PartitionSpec as P

X, Y, Z, CORE = "x", ("grp", "ylo"), "col", "core"
PLANE = ("grp", "x", "ylo", "core")
LOW, F32 = jnp.bfloat16, jnp.float32
def shift(value, axis, size, step):
    return lax.ppermute(value, axis, [(i, (i + step) % size) for i in range(size)])


def along_z(value, *pairs):
    return lax.ppermute(value, Z, pairs)


def swap(value):
    return lax.ppermute(value, CORE, [(0, 1), (1, 0)])


def parts_of(value):
    out = []
    for _ in range(3):
        part = lax.reduce_precision(value, 8, 7)
        out.append(part.astype(LOW))
        value = value - part
    return out


def two_parts(value):
    high = lax.reduce_precision(value, 8, 7)
    return high.astype(LOW), (value - high).astype(LOW)


def body(orbital_b, gaps, block_inverse):
    own, width = orbital_b.shape
    panel = block_inverse.shape[0]
    nx, ny, nz = lax.axis_size(X), lax.axis_size(Y), lax.axis_size(Z)
    x, y, z, core = (lax.axis_index(a) for a in (X, Y, Z, CORE))
    count = width // lax.axis_size(PLANE)
    steps = (0, 2, 1, 3)

    with jax.named_scope("panel_z"):
        piece = orbital_b[:, :panel]
        far_a = along_z(piece, (0, 3))
        far_b = along_z(piece, (0, 6))

    with jax.named_scope("blocks"):
        weight = 2.0 * gaps / (gaps * gaps + 1.0)
        extra = jnp.concatenate(
            [jnp.stack(parts_of(weight)), jnp.zeros((13, own), LOW)], axis=0
        )
        blocks = orbital_b.T.reshape(2, nx, -1, own)

        def rows_of(i):
            block = lax.dynamic_index_in_dim(blocks, i, 1, False).reshape(-1, own)
            return jnp.concatenate([block, extra], axis=0)

        rows = [rows_of((x + k) % nx) for k in steps]
        factors = [rows[0]] + [shift(row, X, nx, k) for row, k in zip(rows[1:], steps[1:])]

    with jax.named_scope("panel_z"):
        far_a, far_b, block_inverse, *_ = lax.optimization_barrier(
            (far_a, far_b, block_inverse, *rows)
        )
        held = jnp.where(z == 3, far_a, jnp.where(z == 6, far_b, piece))
        near_a = along_z(held, (0, 7), (3, 4), (6, 5))
        near_b = along_z(held, (0, 1), (3, 2))
        inv_high, inv_rest = two_parts(block_inverse)
        near_a, near_b, inv_high, inv_rest, *factors = lax.optimization_barrier(
            (near_a, near_b, inv_high, inv_rest, *factors)
        )
        held = jnp.where((z == 7) | (z == 4) | (z == 5), near_a, held)
        held = jnp.where((z == 1) | (z == 2), near_b, held)

    with jax.named_scope("panel_x"):
        blocks = [held] + [shift(held, X, nx, k) for k in steps[1:]]
        panels = jnp.concatenate(blocks, axis=0)

    with jax.named_scope("response"):
        factors = jnp.concatenate(factors, axis=1)
        weight = jnp.sum(factors[-16:-13].astype(F32), axis=0)
        factors = factors[:-16]
        weighted = (weight[:, None] * panels.astype(F32)).astype(LOW)
        by_core = factors.reshape(ny, 2, count, -1)
        theirs, mine = (
            lax.dynamic_index_in_dim(by_core, c, 1, False).reshape(ny * count, -1)
            for c in (1 - core, core)
        )
        sent = jnp.dot(theirs, weighted, preferred_element_type=F32).astype(LOW)
        kept = jnp.dot(mine, weighted, preferred_element_type=F32)
        kept, sent = lax.optimization_barrier((kept, swap(sent)))
        kept = (kept + sent.astype(F32)).reshape(ny, count, panel)
        kept, *blocks = lax.optimization_barrier((kept, *blocks))

    with jax.named_scope("sum_y"):
        total = lax.dynamic_index_in_dim(kept, y, 0, False)
        for k in (2, 1, 3):
            piece = lax.dynamic_index_in_dim(kept, (y + k) % ny, 0, False).astype(LOW)
            total = total + shift(piece, Y, ny, k).astype(F32)

    with jax.named_scope("inverse_factors"):
        panels = jnp.concatenate(blocks, axis=0)
        inverse_factors = sum(
            lax.dot_general(part, panels, (((1,), (1,)), ((), ())), preferred_element_type=F32)
            for part in (inv_high, inv_rest)
        )
        inverse_factors = jnp.concatenate(two_parts(inverse_factors), axis=1)

    with jax.named_scope("screen"):
        place = z * width + lax.axis_index(PLANE) * count
        unit = (lax.iota(jnp.int32, count)[:, None] + place) == lax.iota(jnp.int32, panel)[None, :]
        total = unit.astype(F32) + total
        high, rest = two_parts(total)
        screened = jnp.dot(
            jnp.concatenate([high, rest], axis=0), inv_high, preferred_element_type=F32
        )
        screened = screened[:count] + screened[count:]
        screened = screened + jnp.dot(high, inv_rest, preferred_element_type=F32)

    with jax.named_scope("gather_y"):
        gathered = jnp.concatenate([high] + [shift(high, Y, ny, k) for k in steps[1:]], axis=0)
        gathered, inverse_factors, screened = lax.optimization_barrier(
            (gathered, inverse_factors, screened)
        )
        by_y = factors.reshape(ny, 2, count, -1)
        ordered = [
            jnp.concatenate(
                [
                    lax.dynamic_slice(by_y, ((y - k) % ny, c, 0, 0), (1, 1, count, nx * own))
                    for k in steps
                ]
            ).reshape(-1, nx * own)
            for c in (core, 1 - core)
        ]

    with jax.named_scope("sigma"):

        def terms_of(rows, weights):
            products = jnp.dot(rows, inverse_factors, preferred_element_type=F32)
            weights = jnp.concatenate([weights, weights], axis=1).astype(F32)
            return jnp.sum(products * weights, axis=0)

        local, other = lax.optimization_barrier((terms_of(gathered, ordered[0]), swap(gathered)))
        local = -(local + terms_of(other, ordered[1])).reshape(2, nx, own)
        local = local[0] + local[1]
        back = (x - lax.iota(jnp.int32, nx)) % nx
        by_x = sum(
            jnp.where((back == k)[:, None], local[i][None], 0.0) for i, k in enumerate(steps)
        )
        copies = jnp.broadcast_to(by_x[:, None], (nx, nz, own)).reshape(-1, own)
        terms = lax.all_to_all(copies, (X, Z), 0, 0, tiled=True)
        sigma = jnp.sum(terms, axis=0)
    return sigma, screened[None]


def solution(mesh):
    split = Mesh(mesh.devices.reshape(2, 4, 2, 2, 8), ("grp", "x", "ylo", "core", "col"))
    return jax.shard_map(
        body,
        mesh=split,
        in_specs=(P(PLANE, Z), P(PLANE), P()),
        out_specs=(P(PLANE), P(Z, PLANE, None)),
        check_vma=False,
    )
```

```python
import jax
import jax.numpy as jnp
from jax import lax
from jax.sharding import Mesh, PartitionSpec as P

X, Y, Z, CORE = "x", ("grp", "ylo"), "col", "core"
PLANE = ("grp", "x", "ylo", "core")
LOW, F32 = jnp.bfloat16, jnp.float32
def shift(value, axis, size, step):
    return lax.ppermute(value, axis, [(i, (i + step) % size) for i in range(size)])


def along_z(value, *pairs):
    return lax.ppermute(value, Z, pairs)


def swap(value):
    return lax.ppermute(value, CORE, [(0, 1), (1, 0)])


def parts_of(value):
    out = []
    for _ in range(3):
        part = lax.reduce_precision(value, 8, 7)
        out.append(part.astype(LOW))
        value = value - part
    return out


def two_parts(value):
    high = lax.reduce_precision(value, 8, 7)
    return high.astype(LOW), (value - high).astype(LOW)


def body(orbital_b, gaps, block_inverse):
    own, width = orbital_b.shape
    panel = block_inverse.shape[0]
    nx, ny, nz = lax.axis_size(X), lax.axis_size(Y), lax.axis_size(Z)
    x, y, z, core = (lax.axis_index(a) for a in (X, Y, Z, CORE))
    count = width // lax.axis_size(PLANE)
    steps = (0, 2, 1, 3)

    with jax.named_scope("panel_z"):
        piece = orbital_b[:, :panel]
        far_a = along_z(piece, (0, 3))
        far_b = along_z(piece, (0, 6))

    with jax.named_scope("blocks"):
        weight = 2.0 * gaps / (gaps * gaps + 1.0)
        extra = jnp.concatenate(
            [jnp.stack(parts_of(weight)), jnp.zeros((13, own), LOW)], axis=0
        )
        blocks = orbital_b.T.reshape(2, nx, -1, own)

        def rows_of(i):
            block = lax.dynamic_index_in_dim(blocks, i, 1, False).reshape(-1, own)
            return jnp.concatenate([block, extra], axis=0)

        rows = [rows_of((x + k) % nx) for k in steps]
        factors = [rows[0]] + [shift(row, X, nx, k) for row, k in zip(rows[1:], steps[1:])]

    with jax.named_scope("panel_z"):
        far_a, far_b, block_inverse, *_ = lax.optimization_barrier(
            (far_a, far_b, block_inverse, *rows)
        )
        held = jnp.where(z == 3, far_a, jnp.where(z == 6, far_b, piece))
        near_a = along_z(held, (0, 7), (3, 4), (6, 5))
        near_b = along_z(held, (0, 1), (3, 2))
        inv_high, inv_rest = two_parts(block_inverse)
        near_a, near_b, inv_high, inv_rest, *factors = lax.optimization_barrier(
            (near_a, near_b, inv_high, inv_rest, *factors)
        )
        held = jnp.where((z == 7) | (z == 4) | (z == 5), near_a, held)
        held = jnp.where((z == 1) | (z == 2), near_b, held)

    with jax.named_scope("panel_x"):
        blocks = [held] + [shift(held, X, nx, k) for k in steps[1:]]

    with jax.named_scope("response"):
        factors = jnp.concatenate(factors, axis=1)
        weight = jnp.sum(factors[-16:-13].astype(F32), axis=0)
        factors = factors[:-16]
        by_core = factors.reshape(ny, 2, count, -1)
        theirs, mine = (
            lax.dynamic_index_in_dim(by_core, c, 1, False).reshape(ny * count, -1)
            for c in (1 - core, core)
        )
        split = 2 * own

        def product(rows, part):
            block = jnp.concatenate(blocks[:2] if part == 0 else blocks[2:], axis=0)
            columns = slice(part * split, (part + 1) * split)
            weighted = (weight[columns, None] * block.astype(F32)).astype(LOW)
            return jnp.dot(rows[:, columns], weighted, preferred_element_type=F32)

        early = [product(rows, 0) for rows in (theirs, mine)]
        *early, blocks[2], blocks[3] = lax.optimization_barrier((*early, blocks[2], blocks[3]))
        sent = (early[0] + product(theirs, 1)).astype(LOW)
        kept = early[1] + product(mine, 1)
        kept, sent = lax.optimization_barrier((kept, swap(sent)))
        kept = (kept + sent.astype(F32)).reshape(ny, count, panel)
        kept, *blocks = lax.optimization_barrier((kept, *blocks))

    with jax.named_scope("sum_y"):
        total = lax.dynamic_index_in_dim(kept, y, 0, False)
        for k in (2, 1, 3):
            piece = lax.dynamic_index_in_dim(kept, (y + k) % ny, 0, False).astype(LOW)
            total = total + shift(piece, Y, ny, k).astype(F32)

    with jax.named_scope("inverse_factors"):
        panels = jnp.concatenate(blocks, axis=0)
        inverse_factors = sum(
            lax.dot_general(part, panels, (((1,), (1,)), ((), ())), preferred_element_type=F32)
            for part in (inv_high, inv_rest)
        )
        inverse_factors = jnp.concatenate(two_parts(inverse_factors), axis=1)

    with jax.named_scope("screen"):
        place = z * width + lax.axis_index(PLANE) * count
        unit = (lax.iota(jnp.int32, count)[:, None] + place) == lax.iota(jnp.int32, panel)[None, :]
        total = unit.astype(F32) + total
        high, rest = two_parts(total)
        screened = jnp.dot(
            jnp.concatenate([high, rest], axis=0), inv_high, preferred_element_type=F32
        )
        screened = screened[:count] + screened[count:]
        screened = screened + jnp.dot(high, inv_rest, preferred_element_type=F32)

    with jax.named_scope("gather_y"):
        gathered = jnp.concatenate([high] + [shift(high, Y, ny, k) for k in steps[1:]], axis=0)
        gathered, inverse_factors, screened = lax.optimization_barrier(
            (gathered, inverse_factors, screened)
        )
        by_y = factors.reshape(ny, 2, count, -1)
        ordered = [
            jnp.concatenate(
                [
                    lax.dynamic_slice(by_y, ((y - k) % ny, c, 0, 0), (1, 1, count, nx * own))
                    for k in steps
                ]
            ).reshape(-1, nx * own)
            for c in (core, 1 - core)
        ]

    with jax.named_scope("sigma"):

        def terms_of(rows, weights):
            products = jnp.dot(rows, inverse_factors, preferred_element_type=F32)
            weights = jnp.concatenate([weights, weights], axis=1).astype(F32)
            return jnp.sum(products * weights, axis=0)

        local, other = lax.optimization_barrier((terms_of(gathered, ordered[0]), swap(gathered)))
        local = -(local + terms_of(other, ordered[1])).reshape(2, nx, own)
        local = local[0] + local[1]
        back = (x - lax.iota(jnp.int32, nx)) % nx
        by_x = sum(
            jnp.where((back == k)[:, None], local[i][None], 0.0) for i, k in enumerate(steps)
        )
        copies = jnp.broadcast_to(by_x[:, None], (nx, nz, own)).reshape(-1, own)
        terms = lax.all_to_all(copies, (X, Z), 0, 0, tiled=True)
        sigma = jnp.sum(terms, axis=0)
    return sigma, screened[None]


def solution(mesh):
    split = Mesh(mesh.devices.reshape(2, 4, 2, 2, 8), ("grp", "x", "ylo", "core", "col"))
    return jax.shard_map(
        body,
        mesh=split,
        in_specs=(P(PLANE, Z), P(PLANE), P()),
        out_specs=(P(PLANE), P(Z, PLANE, None)),
        check_vma=False,
    )
```

```python
import jax
import jax.numpy as jnp
from jax import lax
from jax.sharding import Mesh, PartitionSpec as P

X, Y, Z, CORE = "x", ("grp", "ylo"), "col", "core"
PLANE = ("grp", "x", "ylo", "core")
LOW, F32 = jnp.bfloat16, jnp.float32
def shift(value, axis, size, step):
    return lax.ppermute(value, axis, [(i, (i + step) % size) for i in range(size)])


def along_z(value, *pairs):
    return lax.ppermute(value, Z, pairs)


def swap(value):
    return lax.ppermute(value, CORE, [(0, 1), (1, 0)])


def parts_of(value):
    out = []
    for _ in range(3):
        part = lax.reduce_precision(value, 8, 7)
        out.append(part.astype(LOW))
        value = value - part
    return out


def two_parts(value):
    high = lax.reduce_precision(value, 8, 7)
    return high.astype(LOW), (value - high).astype(LOW)


def body(orbital_b, gaps, block_inverse):
    own, width = orbital_b.shape
    panel = block_inverse.shape[0]
    nx, ny, nz = lax.axis_size(X), lax.axis_size(Y), lax.axis_size(Z)
    x, y, z, core = (lax.axis_index(a) for a in (X, Y, Z, CORE))
    count = width // lax.axis_size(PLANE)
    steps = (0, 2, 1, 3)

    with jax.named_scope("panel_z"):
        piece = orbital_b[:, :panel]
        far_a = along_z(piece, (0, 3))
        far_b = along_z(piece, (0, 6))
        orbital_b, far_a, far_b = lax.optimization_barrier((orbital_b, far_a, far_b))

    with jax.named_scope("blocks"):
        weight = 2.0 * gaps / (gaps * gaps + 1.0)
        extra = jnp.concatenate(
            [jnp.stack(parts_of(weight)), jnp.zeros((13, own), LOW)], axis=0
        )
        blocks = orbital_b.T.reshape(2, nx, -1, own)

        def rows_of(i):
            block = lax.dynamic_index_in_dim(blocks, i, 1, False).reshape(-1, own)
            return jnp.concatenate([block, extra], axis=0)

        rows = [rows_of((x + k) % nx) for k in steps]
        factors = [rows[0]] + [shift(row, X, nx, k) for row, k in zip(rows[1:], steps[1:])]

    with jax.named_scope("panel_z"):
        held = jnp.where(z == 3, far_a, jnp.where(z == 6, far_b, piece))
        near_a = along_z(held, (0, 7), (3, 4), (6, 5))
        near_b = along_z(held, (0, 1), (3, 2))
        near_a, near_b, *factors = lax.optimization_barrier((near_a, near_b, *factors))
        held = jnp.where((z == 7) | (z == 4) | (z == 5), near_a, held)
        held = jnp.where((z == 1) | (z == 2), near_b, held)

    with jax.named_scope("panel_x"):
        blocks = [held] + [shift(held, X, nx, k) for k in steps[1:]]
        inv_high, inv_rest = two_parts(block_inverse + 0 * held[:1, :1].astype(F32))
        blocks[2], inv_high, inv_rest = lax.optimization_barrier((blocks[2], inv_high, inv_rest))
        panels = jnp.concatenate(blocks, axis=0)

    with jax.named_scope("response"):
        factors = jnp.concatenate(factors, axis=1)
        weight = jnp.sum(factors[-16:-13].astype(F32), axis=0)
        factors = factors[:-16]
        weighted = (weight[:, None] * panels.astype(F32)).astype(LOW)
        by_core = factors.reshape(ny, 2, count, -1)
        theirs, mine = (
            lax.dynamic_index_in_dim(by_core, c, 1, False).reshape(ny * count, -1)
            for c in (1 - core, core)
        )
        sent = jnp.dot(theirs, weighted, preferred_element_type=F32).astype(LOW)
        kept = jnp.dot(mine, weighted, preferred_element_type=F32)
        kept, sent = lax.optimization_barrier((kept, swap(sent)))
        kept = (kept + sent.astype(F32)).reshape(ny, count, panel)
        kept, *blocks = lax.optimization_barrier((kept, *blocks))

    with jax.named_scope("sum_y"):
        total = lax.dynamic_index_in_dim(kept, y, 0, False)
        for k in (2, 1, 3):
            piece = lax.dynamic_index_in_dim(kept, (y + k) % ny, 0, False).astype(LOW)
            total = total + shift(piece, Y, ny, k).astype(F32)

    with jax.named_scope("inverse_factors"):
        panels = jnp.concatenate(blocks, axis=0)
        inverse_factors = sum(
            lax.dot_general(part, panels, (((1,), (1,)), ((), ())), preferred_element_type=F32)
            for part in (inv_high, inv_rest)
        )
        inverse_factors = jnp.concatenate(two_parts(inverse_factors), axis=1)

    with jax.named_scope("screen"):
        place = z * width + lax.axis_index(PLANE) * count
        unit = (lax.iota(jnp.int32, count)[:, None] + place) == lax.iota(jnp.int32, panel)[None, :]
        total = unit.astype(F32) + total
        high, rest = two_parts(total)
        screened = jnp.dot(
            jnp.concatenate([high, rest], axis=0), inv_high, preferred_element_type=F32
        )
        screened = screened[:count] + screened[count:]
        screened = screened + jnp.dot(high, inv_rest, preferred_element_type=F32)

    with jax.named_scope("gather_y"):
        gathered = jnp.concatenate([high] + [shift(high, Y, ny, k) for k in steps[1:]], axis=0)
        gathered, inverse_factors, screened = lax.optimization_barrier(
            (gathered, inverse_factors, screened)
        )
        by_y = factors.reshape(ny, 2, count, -1)
        ordered = [
            jnp.concatenate(
                [
                    lax.dynamic_slice(by_y, ((y - k) % ny, c, 0, 0), (1, 1, count, nx * own))
                    for k in steps
                ]
            ).reshape(-1, nx * own)
            for c in (core, 1 - core)
        ]

    with jax.named_scope("sigma"):

        def terms_of(rows, weights):
            products = jnp.dot(rows, inverse_factors, preferred_element_type=F32)
            weights = jnp.concatenate([weights, weights], axis=1).astype(F32)
            return jnp.sum(products * weights, axis=0)

        local, other = lax.optimization_barrier((terms_of(gathered, ordered[0]), swap(gathered)))
        local = -(local + terms_of(other, ordered[1])).reshape(2, nx, own)
        local = local[0] + local[1]
        back = (x - lax.iota(jnp.int32, nx)) % nx
        by_x = sum(
            jnp.where((back == k)[:, None], local[i][None], 0.0) for i, k in enumerate(steps)
        )
        copies = jnp.broadcast_to(by_x[:, None], (nx, nz, own)).reshape(-1, own)
        terms = lax.all_to_all(copies, (X, Z), 0, 0, tiled=True)
        sigma = jnp.sum(terms, axis=0)
    return sigma, screened[None]


def solution(mesh):
    split = Mesh(mesh.devices.reshape(2, 4, 2, 2, 8), ("grp", "x", "ylo", "core", "col"))
    return jax.shard_map(
        body,
        mesh=split,
        in_specs=(P(PLANE, Z), P(PLANE), P()),
        out_specs=(P(PLANE), P(Z, PLANE, None)),
        check_vma=False,
    )
```
